128 devices in a mesh: member: 8 (over x, core), node: 16 (over z, y).
Axes of the slice: x: 4, y: 4, z: 4, core: 2. Of those that a mesh axis runs over, the one named last changes fastest.
Arguments:
- latents: bfloat16 [8, 6144, 1024], P('member', 'node'), may hold values from -6 to 6
- grid_embed: bfloat16 [16384, 1024], P('node'), may hold values from -6 to 6
- neighbours: int32 [3, 16384], P(None, 'node'), may hold values from 0 to 383
- edge_coef: float32 [3, 16384], P(None, 'node'), may hold values from 0.1 to 1
- w_value: bfloat16 [1024, 1024], replicated, may hold values from -0.1875 to 0.1875
- gain: float32 [1024], replicated, may hold values from 0.25 to 1.75
- w_hidden: bfloat16 [1024, 2048], replicated, may hold values from -0.1875 to 0.1875
- output_weight: bfloat16 [100, 2048], replicated, may hold values from -0.125 to 0.125
- targets: float32 [100, 16384], P(None, 'node'), may hold values from -6 to 6
- var_weight: float32 [100], replicated, may hold values from 0.2 to 2
- area: float32 [16384], P('node'), may hold values from 0.3 to 3
- valid_counts: int32 [16], replicated, may hold values from 512 to 1024, as said below
Outputs:
- grad_value: float32 [1024, 1024], P(('member', 'node'))
- grad_gain: float32 [1024], P(('member', 'node'))
- grad_hidden: float32 [1024, 2048], P(('member', 'node'))
- grad_out: float32 [100, 2048], P(None, ('member', 'node'))
- grad_latents: bfloat16 [8, 6144, 1024], P('member', 'node')
The draws below stay inside these ranges and needn't reach their ends.
Inputs may be any that keep to these rules, and one draw needn't show every extreme that they name: `neighbours`: an entry n in column g of partition p names mesh node p * 384 + n. `valid_counts`: some partition has all 1024 slots valid and some exactly half of them.
All inputs are finite; a program needn't handle non-finite values.
Results may differ from the reference program's by a relative error of at most 0.012.
Values may be sent and summed in bfloat16 or wider, within the bound.
No kernel may reach another device: no remote copies, remote signals or barrier semaphores. Data moves between devices by JAX's collectives and lax.ppermute only.
A program may use at most 128 MiB of HBM per device.

```python
import math
import jax
import jax.numpy as jnp
from jax import lax

D = 1024
HID = 2048
VARS = 100
K = 3
NODES_DEV = 384
GRID_DEV = 1024
MEMBERS = 8
PARTS_SIZE = 16
NODES = 6144
GRID = 16384


def draw_valid_counts(key, part):
    key = jax.random.fold_in(key, 7)
    first_key, second_key = jax.random.split(key)
    counts = jax.random.randint(first_key, (PARTS_SIZE,), GRID_DEV // 2, GRID_DEV + 1)
    order = jax.random.permutation(second_key, PARTS_SIZE)
    positions = jnp.arange(PARTS_SIZE)
    counts = jnp.where(positions == order[0], GRID_DEV, counts)
    counts = jnp.where(positions == order[1], GRID_DEV // 2, counts)
    return counts.astype(jnp.int32)


def set_ends(values, own_key, smallest, high):
    longest = values.shape.index(max(values.shape))
    spots = []
    for shift in (0, 1):
        where = [jax.random.randint(jax.random.fold_in(own_key, axis), (), 0, length) for axis, length in enumerate(values.shape)]
        where[longest] = (where[longest] + shift) % values.shape[longest]
        spots.append(tuple(where))
    return values.at[spots[0]].set(smallest).at[spots[1]].set(high)


def levels(stream_key, dims, cuts, least, high):
    factor_of, own = 1.0, jax.random.fold_in(stream_key, 6)
    for position, parts in cuts:
        steps = jnp.exp(jax.random.uniform(jax.random.fold_in(own, position), (parts,), jnp.float32, least / len(cuts), high / len(cuts)))
        factor_of = factor_of * jnp.repeat(steps, dims[position] // parts).reshape([-1 if axis == position else 1 for axis in range(len(dims))])
    return factor_of


def scatter_about(rng, dims, deviation, most, pieces=(), kind=jnp.bfloat16):
    level = levels(rng, dims, pieces, -0.22, 0.18) if pieces else 1.0
    entries = jax.random.normal(rng, dims, jnp.float32) * deviation * level
    return jnp.minimum(jnp.maximum(entries, -most), most).astype(kind)


def setup_inputs(seed: int = 0) -> dict:
    seeds = jax.random.split(jax.random.key(seed), 13)
    latents = scatter_about(seeds[0], (MEMBERS, NODES, D), 1.0, 6.0, ((0, 8), (1, 16)))
    grid_embed = scatter_about(seeds[1], (GRID, D), 1.0, 6.0, ((0, 16),))
    neighbours = set_ends(jax.random.randint(seeds[2], (K, GRID), 0, NODES_DEV), jax.random.fold_in(seeds[2], 1), 0, NODES_DEV - 1).astype(jnp.int32)
    edge_coef = jnp.clip(jnp.exp(math.log(1.0) - 2.3025851 * jax.random.uniform(seeds[3], (K, GRID), jnp.float32) ** levels(seeds[3], (K, GRID), ((1, 16),), -0.2, 0.2)), 0.1, 1.0)
    w_value = scatter_about(seeds[4], (D, D), D ** -0.5, 0.1875)
    gain = jnp.clip(1.0 + 0.15 * jax.random.normal(seeds[5], (D,), jnp.float32), 0.25, 1.75)
    w_hidden = scatter_about(seeds[6], (D, HID), D ** -0.5, 0.1875)
    output_weight = scatter_about(seeds[7], (VARS, HID), HID ** -0.5, 0.125)
    targets = scatter_about(seeds[8], (VARS, GRID), 1.0, 6.0, ((1, 16),), jnp.float32)
    var_weight = jnp.clip(jnp.exp(jax.random.uniform(seeds[9], (VARS,), jnp.float32, math.log(0.2), math.log(2.0))), 0.2, 2.0)
    area = jnp.clip(jnp.exp(math.log(3.0) - 2.3025851 * jax.random.uniform(seeds[10], (GRID,), jnp.float32) ** levels(seeds[10], (GRID,), ((0, 16),), -0.2, 0.2)), 0.3, 3.0)
    valid_counts = draw_valid_counts(jax.random.fold_in(seeds[12], 71), 0)
    return {"latents": latents, "grid_embed": grid_embed, "neighbours": neighbours, "edge_coef": edge_coef, "w_value": w_value, "gain": gain, "w_hidden": w_hidden, "output_weight": output_weight, "targets": targets, "var_weight": var_weight, "area": area, "valid_counts": valid_counts}


kernel_width = 0.25
fair_alpha = 0.95
norm_eps = 1e-05

def decode_forward(latent_rows, embedded, neighbour_rows, coef_rows, w_value, gain, w_hidden, output_weight):
    node_values = jnp.dot(latent_rows, w_value, preferred_element_type=jnp.float32).astype(jnp.bfloat16)
    gathered = node_values[neighbour_rows]
    message = lax.optimization_barrier(jnp.sum(coef_rows[:, :, None] * gathered.astype(jnp.float32), axis=0))
    summed = embedded.astype(jnp.float32) + message
    inverse_root_mean_square = lax.rsqrt(lax.optimization_barrier(jnp.mean(summed * summed, axis=-1, keepdims=True)) + norm_eps)
    unit_norm_rows = summed * inverse_root_mean_square
    normalized_rows = (unit_norm_rows * gain).astype(jnp.bfloat16)
    preactivation = jnp.dot(normalized_rows, w_hidden, preferred_element_type=jnp.float32)
    hidden_activation = jax.nn.gelu(preactivation).astype(jnp.bfloat16)
    member_prediction = lax.dot_general(output_weight, hidden_activation, (((1,), (1,)), ((), ())), preferred_element_type=jnp.float32)
    return (member_prediction, (unit_norm_rows, inverse_root_mean_square, normalized_rows, preactivation, hidden_activation))

def ensemble_terms(member_own_field, ensemble, target_row_values, weight_matrix):
    member_count = ensemble.shape[0]
    misfit = member_own_field - target_row_values
    distance = jnp.sqrt(misfit * misfit + kernel_width * kernel_width)
    deltas = member_own_field[None] - ensemble
    pair_dist = jnp.sqrt(deltas * deltas + kernel_width * kernel_width)
    spread = (1.0 - (1.0 - fair_alpha) / member_count) / (2.0 * member_count * (member_count - 1))
    activation_slopes = misfit / distance / member_count - 2.0 * spread * lax.optimization_barrier(jnp.sum(deltas / pair_dist, axis=0))
    return weight_matrix * activation_slopes

def backward_upper(slope_rows, saved_tensors, w_hidden, output_weight):
    unit_norm_rows, inverse_root_mean_square, normalized_rows, preactivation, hidden_activation = saved_tensors
    grad_out = jnp.dot(slope_rows, hidden_activation, preferred_element_type=jnp.float32)
    hidden_grad = lax.dot_general(slope_rows, output_weight, (((0,), (0,)), ((), ())), preferred_element_type=jnp.float32)
    _, gelu_back = jax.vjp(jax.nn.gelu, preactivation)
    pre_grad = gelu_back(hidden_grad)[0].astype(jnp.bfloat16)
    grad_hidden = lax.dot_general(normalized_rows, pre_grad, (((0,), (0,)), ((), ())), preferred_element_type=jnp.float32)
    normed_grad = lax.dot_general(pre_grad, w_hidden, (((1,), (1,)), ((), ())), preferred_element_type=jnp.float32)
    return (grad_out, grad_hidden, normed_grad)

def backward_lower(normed_grad, saved_tensors, latent_rows, neighbour_rows, coef_rows, w_value, gain):
    unit_norm_rows, inverse_root_mean_square, normalized_rows, preactivation, hidden_activation = saved_tensors
    grad_gain = lax.optimization_barrier(jnp.sum(normed_grad * unit_norm_rows, axis=0))
    unit_grad = normed_grad * gain
    summed_grad = inverse_root_mean_square * (unit_grad - unit_norm_rows * lax.optimization_barrier(jnp.mean(unit_grad * unit_norm_rows, axis=-1, keepdims=True)))
    edge_grads = coef_rows[:, :, None] * summed_grad[None]
    width = summed_grad.shape[1]
    value_grad = jax.ops.segment_sum(edge_grads.reshape(-1, width), neighbour_rows.reshape(-1), num_segments=latent_rows.shape[0]).astype(jnp.bfloat16)
    grad_value = lax.dot_general(latent_rows, value_grad, (((0,), (0,)), ((), ())), preferred_element_type=jnp.float32)
    latent_grad = lax.dot_general(value_grad, w_value, (((1,), (1,)), ((), ())), preferred_element_type=jnp.float32).astype(jnp.bfloat16)
    return (grad_value, grad_gain, latent_grad)

def reference(latents, grid_embed, neighbours, edge_coef, w_value, gain, w_hidden, output_weight, targets, var_weight, area, valid_counts):
    latent_parts = latents.reshape(MEMBERS, PARTS_SIZE, NODES_DEV, D).transpose(1, 0, 2, 3)
    embed_parts = grid_embed.reshape(PARTS_SIZE, GRID_DEV, D)
    neighbour_parts = neighbours.reshape(K, PARTS_SIZE, GRID_DEV).transpose(1, 0, 2)
    coef_parts = edge_coef.reshape(K, PARTS_SIZE, GRID_DEV).transpose(1, 0, 2)
    target_parts = targets.reshape(VARS, PARTS_SIZE, GRID_DEV).transpose(1, 0, 2)
    area_parts = area.reshape(PARTS_SIZE, GRID_DEV)

    def one_part(carry, part_data):
        ensemble_latents, embedded, neighbour_rows, coef_rows, target_row_values, area_rows, live_count = part_data

        def execute_forward(latent_rows):
            return decode_forward(latent_rows, embedded, neighbour_rows, coef_rows, w_value, gain, w_hidden, output_weight)
        member_prediction, saved_tensors = jax.vmap(execute_forward)(ensemble_latents)
        live = (jnp.arange(GRID_DEV) < live_count).astype(jnp.float32)
        weight_matrix = var_weight[:, None] * (area_rows * live)[None, :] / VARS
        activation_slopes = jax.vmap(lambda member_own_field: ensemble_terms(member_own_field, member_prediction, target_row_values, weight_matrix))(member_prediction)

        def run_backward(slope_rows, latent_rows, member_stored):
            grad_out, grad_hidden, normed_grad = backward_upper(slope_rows, member_stored, w_hidden, output_weight)
            grad_value, grad_gain, latent_grad = backward_lower(normed_grad, member_stored, latent_rows, neighbour_rows, coef_rows, w_value, gain)
            return (grad_value, grad_gain, grad_hidden, grad_out, latent_grad)
        grad_value, grad_gain, grad_hidden, grad_out, latent_grad = jax.vmap(run_backward)(activation_slopes.astype(jnp.bfloat16), ensemble_latents, saved_tensors)
        value_sum, gain_sum, hidden_sum, out_sum = carry
        carry = (value_sum + lax.optimization_barrier(jnp.sum(grad_value, axis=0)), gain_sum + lax.optimization_barrier(jnp.sum(grad_gain, axis=0)), hidden_sum + lax.optimization_barrier(jnp.sum(grad_hidden, axis=0)), out_sum + lax.optimization_barrier(jnp.sum(grad_out, axis=0)))
        return (carry, latent_grad)
    init = (jnp.zeros((D, D), jnp.float32), jnp.zeros((D,), jnp.float32), jnp.zeros((D, HID), jnp.float32), jnp.zeros((VARS, HID), jnp.float32))
    sums, latent_grads = lax.scan(one_part, init, (latent_parts, embed_parts, neighbour_parts, coef_parts, target_parts, area_parts, valid_counts))
    grad_value, grad_gain, grad_hidden, grad_out = sums
    grad_latents = latent_grads.transpose(1, 0, 2, 3).reshape(MEMBERS, NODES, D)
    return (grad_value, grad_gain, grad_hidden, grad_out, grad_latents)
```

```python
import itertools

import jax
import jax.numpy as jnp
from jax import lax
from jax.experimental import pallas as pl
from jax.experimental.pallas import tpu as pltpu
from jax.sharding import PartitionSpec as P

BF = jnp.bfloat16
F32 = jnp.float32
kernel_width = 0.25
fair_alpha = 0.95
norm_eps = 1e-05
members = 8
GELU_C = 0.7978845608028654
VMEM = 56 * 1024 * 1024
ORDER_A1 = "xzy"
ORDER_A2 = "zyx"
ORDER_B = "yxz"
AXES = ("member", "node")


def flat(x, c, z, y):
    return ((x * 2 + c) * 4 + z) * 4 + y


def core_pairs():
    return [
        (flat(x, c, z, y), flat(x, 1 - c, z, y))
        for x, c, z, y in itertools.product(range(4), range(2), range(4), range(4))
    ]


def ring_pairs(axis, step):
    pairs = []
    for x, c, z, y in itertools.product(range(4), range(2), range(4), range(4)):
        to = {"x": x, "z": z, "y": y}
        to[axis] ^= (1, 3)[c ^ step]
        pairs.append((flat(x, c, z, y), flat(to["x"], c, to["z"], to["y"])))
    return pairs


def own_place():
    member, node = lax.axis_index("member"), lax.axis_index("node")
    return {"x": member // 2, "c": member % 2, "z": node // 4, "y": node % 4}


def shard_at(position, own, order):
    core = own["c"] ^ ((position >> 6) & 1)
    first, second = 1 + 2 * core, 3 - 2 * core
    place = {}
    for t, axis in enumerate(order):
        a, b = (position >> (5 - 2 * t)) & 1, (position >> (4 - 2 * t)) & 1
        place[axis] = own[axis] ^ (a * first) ^ (b * second)
    return flat(place["x"], core, place["z"], place["y"])


def points_at(position, own):
    core = own["c"] ^ (position >> 2)
    first, second = 1 + 2 * core, 3 - 2 * core
    x = own["x"] ^ (((position >> 1) & 1) * first) ^ ((position & 1) * second)
    return x * 2 + core


def dot(a, b, dims=((1,), (0,))):
    return lax.dot_general(a, b, (dims, ((), ())), preferred_element_type=F32)


def reorder(source, target, own, order, columns=None):
    def body(q, carry):
        blocks = []
        for k in range(2):
            shard = shard_at(2 * q + k, own, order)
            blocks.append(source[pl.ds(pl.multiple_of(shard * 8, 8), 8), :])
        rows = pl.ds(pl.multiple_of(q * 16, 16), 16)
        target[rows, :] = jnp.concatenate(blocks, axis=0).astype(BF)
        return carry

    lax.fori_loop(0, 64, body, 0, unroll=4)


def forward_kernel(
    lat_ref, wv_ref, nb_ref, cf_ref, emb_ref, gain_ref, wh_ref, ow_ref,
    fc_ref, hid_ref, dg_ref, nta_ref, ntb_ref, unit_ref, inv_ref, st_ref,
    nrm, total, turned,
):
    j = pl.program_id(0)
    nodes, points = st_ref.shape
    own = own_place()

    @pl.when(j == 0)
    def _():
        values = dot(lat_ref[...], wv_ref[...]).astype(BF)
        rows_of = lax.broadcasted_iota(jnp.int32, (nodes, 256), 0)
        for r in range(points // 256):
            rows = slice(256 * r, 256 * r + 256)
            st = jnp.zeros((nodes, 256), F32)
            for k in range(3):
                st = st + jnp.where(nb_ref[k : k + 1, rows] == rows_of, cf_ref[k : k + 1, rows], 0.0)
            st = st.astype(BF)
            st_ref[:, rows] = st
            summed = emb_ref[rows, :].astype(F32) + dot(st, values, ((0,), (0,)))
            inv = lax.rsqrt(jnp.mean(summed * summed, axis=-1, keepdims=True) + norm_eps)
            unit = summed * inv
            inv_ref[rows, :] = inv
            unit_ref[rows, :] = unit.astype(BF)
            normed = (unit * gain_ref[...]).astype(BF)
            nrm[rows, :] = normed
            turned[:, rows] = normed.astype(F32).T
        reorder(turned, nta_ref, own, ORDER_A1)
        reorder(turned, ntb_ref, own, ORDER_A2)
        total[...] = jnp.zeros_like(total)

    step = 256
    for r in range(points // step):
        rows = slice(step * r, step * r + step)
        pre = dot(nrm[rows, :], wh_ref[...])
        square = pre * pre
        t = jnp.tanh(GELU_C * pre * (1.0 + 0.044715 * square))
        cdf = 0.5 + 0.5 * t
        slope = cdf + 0.5 * GELU_C * pre * (1.0 - t * t) * (1.0 + 3 * 0.044715 * square)
        hid_ref[rows, :] = (pre * cdf).astype(BF)
        dg_ref[rows, :] = slope.astype(BF)
    total[0:100, :] += dot(ow_ref[...], hid_ref[...], ((1,), (1,)))

    @pl.when(j == pl.num_programs(0) - 1)
    def _():
        for p in range(8):
            first = pl.multiple_of(points_at(p, own) * 128, 128)
            fc_ref[p] = total[:, pl.ds(first, 128)]


def slopes_kernel(vc_ref, f_ref, r0_ref, r1_ref, r2_ref, tg_ref, vw_ref, area_ref, keep_ref, send_ref, held):
    member, node = lax.axis_index("member"), lax.axis_index("node")
    first = pl.multiple_of(member * 128, 128)
    mine = pl.ds(first, 128)
    place = first + lax.broadcasted_iota(jnp.int32, (1, 128), 1)
    live = jnp.where(place < vc_ref[node], area_ref[:, mine], 0.0)
    spread = (1.0 - (1.0 - fair_alpha) / members) / (2.0 * members * (members - 1))
    fields = [
        f_ref.at[0], r0_ref.at[0], r1_ref.at[0], r1_ref.at[2],
        r2_ref.at[0], r2_ref.at[1], r2_ref.at[2], r2_ref.at[3],
    ]
    held[:, 96:112, :] = jnp.zeros((8, 16, 128), F32)
    for top in range(0, 100, 8):
        rows = slice(top, min(top + 8, 100))
        f = [field[rows, :] for field in fields]
        sums = [jnp.zeros_like(f[0]) for _ in f]
        for a in range(8):
            for b in range(a + 1, 8):
                d = f[a] - f[b]
                s = d * lax.rsqrt(d * d + kernel_width * kernel_width)
                sums[a] = sums[a] + s
                sums[b] = sums[b] - s
        target = tg_ref[rows, mine]
        weight = vw_ref[rows, :] * live * 0.01
        for a in range(8):
            d = f[a] - target
            s = d * lax.rsqrt(d * d + kernel_width * kernel_width)
            held[a, rows, :] = weight * (s * (1.0 / members) - 2.0 * spread * sums[a])
    for a in range(4):
        keep_ref[a] = held[a].astype(BF)
        send_ref[a] = held[4 + a].astype(BF)


def upper_kernel(last_piece, *refs):
    if last_piece:
        (s0, s1, s2, s3, ow_ref, dg_ref, hid_ref, nt_ref, go_first,
         pg_ref, keep_ref, send_ref, slopes, turned, own_w, go, go_turned) = refs
    else:
        (s0, s1, s2, s3, ow_ref, dg_ref, hid_ref, nt_ref,
         pg_ref, keep_ref, send_ref, go, slopes, turned, own_w) = refs
    j = pl.program_id(0)
    points = dg_ref.shape[0]
    half = keep_ref.shape[0]
    own = own_place()

    @pl.when(j == 0)
    def _():
        parts = [s0.at[0], s1.at[0], s2.at[0], s2.at[2], s3.at[0], s3.at[1], s3.at[2], s3.at[3]]
        for p in range(8):
            block = jnp.concatenate([parts[p][...].astype(F32), jnp.zeros((16, 128), F32)], axis=0)
            at = pl.ds(pl.multiple_of(points_at(p, own) * 128, 128), 128)
            slopes[:, at] = block.astype(BF)
            turned[at, :] = block.T.astype(BF)
        own_w[...] = jnp.zeros_like(own_w)

    def tile():
        own_w[0:100, :] = ow_ref[...]
        for r in range(points // 256):
            rows = slice(256 * r, 256 * r + 256)
            grad = dot(turned[rows, :], own_w[...])
            pg_ref[rows, :] = (dg_ref[rows, :].astype(F32) * grad).astype(BF)
        go[:, pl.ds(pl.multiple_of(j * 256, 256), 256)] = dot(slopes[...], hid_ref[...])
        keep_ref[...] = dot(nt_ref[0:half, :], pg_ref[...]).astype(BF)
        send_ref[...] = dot(nt_ref[half:, :], pg_ref[...]).astype(BF)

    if not last_piece:
        tile()
        return

    pl.when(j < 4)(tile)

    @pl.when(j == 4)
    def _():
        go_turned[0:1024, :] = go_first[...].T
        go_turned[1024:2048, :] = go[...].T
        for ref, start in ((keep_ref, 0), (send_ref, 64)):

            def body(q, carry, ref=ref, start=start):
                blocks = []
                for k in range(2):
                    shard = shard_at(start + 2 * q + k, own, ORDER_A2)
                    block = go_turned[pl.ds(pl.multiple_of(shard * 16, 16), 16), :]
                    blocks.append(jnp.concatenate([block[0:8], block[8:16]], axis=1))
                rows = pl.ds(pl.multiple_of(q * 16, 16), 16)
                ref[rows, :] = jnp.concatenate(blocks, axis=0).astype(BF)
                return carry

            lax.fori_loop(0, 32, body, 0, unroll=4)


def lower_kernel(
    pga_ref, pgb_ref, wh_ref, unit_ref, inv_ref, gain_ref, st_ref, lat_ref, wv_ref,
    keep_ref, send_ref, gl_ref,
    gain_sum, value_sum, turned, lat_turned, gain_turned, placed,
):
    j = pl.program_id(0)
    width = lat_ref.shape[1]
    half = keep_ref.shape[0]
    own = own_place()

    @pl.when(j == 0)
    def _():
        gain_sum[...] = jnp.zeros_like(gain_sum)
        value_sum[...] = jnp.zeros_like(value_sum)
        turned[...] = lat_ref[...].astype(F32).T
        reorder(turned, lat_turned, own, ORDER_B)

    normed_grad = dot(pga_ref[...], wh_ref[:, 0:1024], ((1,), (1,)))
    normed_grad = normed_grad + dot(pgb_ref[...], wh_ref[:, 1024:2048], ((1,), (1,)))
    unit = unit_ref[...].astype(F32)
    product = normed_grad * unit
    gain_sum[...] += jnp.sum(product, axis=0, keepdims=True)
    mean = jnp.mean(product * gain_ref[...], axis=-1, keepdims=True)
    summed_grad = inv_ref[...] * (normed_grad * gain_ref[...] - unit * mean)
    value_sum[...] += dot(st_ref[...], summed_grad.astype(BF))

    @pl.when(j == pl.num_programs(0) - 1)
    def _():
        value_grad = value_sum[...].astype(BF)
        keep_ref[:, 0:width] = dot(lat_turned[0:half, :], value_grad).astype(BF)
        send_ref[:, 0:width] = dot(lat_turned[half:, :], value_grad).astype(BF)
        gain_turned[...] = jnp.broadcast_to(gain_sum[...], (128, width)).T
        reorder(gain_turned, placed, own, ORDER_B)
        keep_ref[:, width:] = placed[0:half, :]
        send_ref[:, width:] = placed[half:, :]
        gl_ref[...] = dot(value_grad, wv_ref[...], ((1,), (1,))).astype(BF)


def whole(shape):
    return pl.BlockSpec(shape, lambda j: (0,) * len(shape))


def params():
    return pltpu.CompilerParams(vmem_limit_bytes=VMEM, dimension_semantics=("arbitrary",))


def cost(flops, moved):
    return pl.CostEstimate(flops=flops, bytes_accessed=moved, transcendentals=0)


def forward(lat, wv, nb, cf, emb, gain, wh, ow):
    nodes, width = lat.shape
    points = emb.shape[0]
    hidden = wh.shape[1]
    tile = pl.BlockSpec((points, 256), lambda j: (0, j))
    return pl.pallas_call(
        forward_kernel,
        grid=(hidden // 256,),
        in_specs=[
            whole(lat.shape), whole(wv.shape), whole(nb.shape), whole(cf.shape), whole(emb.shape), whole(gain.shape),
            pl.BlockSpec((width, 256), lambda j: (0, j)),
            pl.BlockSpec((ow.shape[0], 256), lambda j: (0, j)),
        ],
        out_specs=[
            whole((8, 104, 128)), tile, tile, whole((width, points)), whole((width, points)),
            whole((points, width)), whole((points, 1)), whole((nodes, points)),
        ],
        out_shape=[
            jax.ShapeDtypeStruct((8, 104, 128), F32),
            jax.ShapeDtypeStruct((points, hidden), BF),
            jax.ShapeDtypeStruct((points, hidden), BF),
            jax.ShapeDtypeStruct((width, points), BF),
            jax.ShapeDtypeStruct((width, points), BF),
            jax.ShapeDtypeStruct((points, width), BF),
            jax.ShapeDtypeStruct((points, 1), F32),
            jax.ShapeDtypeStruct((nodes, points), BF),
        ],
        scratch_shapes=[
            pltpu.VMEM((points, width), BF),
            pltpu.VMEM((104, points), F32),
            pltpu.VMEM((width, points), F32),
        ],
        compiler_params=params(),
        cost_estimate=cost(6_400_000_000, 30_000_000),
        name="forward",
    )(lat, wv, nb, cf, emb, gain, wh, ow)


def slopes_of(vc, f, r0, r1, r2, targets, vw, area):
    vm = pl.BlockSpec(memory_space=pltpu.VMEM)
    return pl.pallas_call(
        slopes_kernel,
        in_specs=[pl.BlockSpec(memory_space=pltpu.SMEM)] + [vm] * 7,
        out_specs=[vm, vm],
        out_shape=[jax.ShapeDtypeStruct((4, 112, 128), BF)] * 2,
        scratch_shapes=[pltpu.VMEM((8, 112, 128), F32)],
        compiler_params=pltpu.CompilerParams(vmem_limit_bytes=VMEM),
        cost_estimate=cost(20_000_000, 3_000_000),
        name="slopes",
    )(vc, f, r0, r1, r2, targets, vw, area)


def upper(last_piece, parts, ow, dg, hid, nt, go_first=None):
    points = dg.shape[0]
    width = nt.shape[0]
    first = 4 if last_piece else 0
    tiles = 5 if last_piece else 4
    col = (lambda j: (0, jnp.minimum(j, 3) + first)) if last_piece else (lambda j: (0, j))
    pg_col = (lambda j: (0, jnp.minimum(j, 3))) if last_piece else (lambda j: (0, j))
    piece = pl.BlockSpec((width // 2, 256), lambda j: (0, j))
    in_specs = [whole(p.shape) for p in parts] + [
        pl.BlockSpec((ow.shape[0], 256), col),
        pl.BlockSpec((points, 256), col),
        pl.BlockSpec((points, 256), col),
        whole(nt.shape),
    ]
    out_specs = [pl.BlockSpec((points, 256), pg_col), piece, piece]
    out_shape = [
        jax.ShapeDtypeStruct((points, 1024), BF),
        jax.ShapeDtypeStruct((width // 2, 256 * tiles), BF),
        jax.ShapeDtypeStruct((width // 2, 256 * tiles), BF),
    ]
    scratch = [pltpu.VMEM((128, points), BF), pltpu.VMEM((points, 128), BF), pltpu.VMEM((128, 256), BF)]
    args = [*parts, ow, dg, hid, nt]
    if last_piece:
        in_specs.append(whole(go_first.shape))
        args.append(go_first)
        scratch += [pltpu.VMEM((128, 1024), F32), pltpu.VMEM((2048, 128), F32)]
    else:
        out_specs.append(whole((128, 1024)))
        out_shape.append(jax.ShapeDtypeStruct((128, 1024), F32))
    return pl.pallas_call(
        lambda *refs: upper_kernel(last_piece, *refs),
        grid=(tiles,),
        in_specs=in_specs,
        out_specs=out_specs,
        out_shape=out_shape,
        scratch_shapes=scratch,
        compiler_params=params(),
        cost_estimate=cost(2_700_000_000, 12_000_000),
        name="upper_second" if last_piece else "upper_first",
    )(*args)


def lower(pga, pgb, wh, unit, inv, gain, st, lat, wv):
    points, width = unit.shape
    nodes = lat.shape[0]
    step = 256
    rows = lambda n: pl.BlockSpec((step, n), lambda j: (j, 0))
    return pl.pallas_call(
        lower_kernel,
        grid=(points // step,),
        in_specs=[
            rows(1024), rows(1024), whole(wh.shape), rows(width), rows(1), whole(gain.shape),
            pl.BlockSpec((nodes, step), lambda j: (0, j)), whole(lat.shape), whole(wv.shape),
        ],
        out_specs=[whole((width // 2, width + 128)), whole((width // 2, width + 128)), whole((nodes, width))],
        out_shape=[
            jax.ShapeDtypeStruct((width // 2, width + 128), BF),
            jax.ShapeDtypeStruct((width // 2, width + 128), BF),
            jax.ShapeDtypeStruct((nodes, width), BF),
        ],
        scratch_shapes=[
            pltpu.VMEM((1, width), F32),
            pltpu.VMEM((nodes, width), F32),
            pltpu.VMEM((width, nodes), F32),
            pltpu.VMEM((width, nodes), BF),
            pltpu.VMEM((width, 128), F32),
            pltpu.VMEM((width, 128), BF),
        ],
        compiler_params=params(),
        cost_estimate=cost(6_700_000_000, 16_000_000),
        name="lower",
    )(pga, pgb, wh, unit, inv, gain, st, lat, wv)


def permute(value, pairs):
    return lax.ppermute(value, AXES, pairs)


def summed_shard(keep, send, order):
    parts = [keep, permute(send, core_pairs())]
    rows = keep.shape[0]
    for axis in order:
        for step in range(2):
            rows //= 2
            out = sum(part[rows : 2 * rows].astype(F32) for part in parts).astype(BF)
            parts = [part[:rows] for part in parts] + [permute(out, ring_pairs(axis, step))]
    return sum(part.astype(F32) for part in parts)


def per_device(
    latents, grid_embed, neighbours, edge_coef, w_value, gain, w_hidden, output_weight,
    targets, var_weight, area, valid_counts,
):
    lat = latents[0]
    gain_row = gain[None, :]
    f, hid, dg, nta, ntb, unit, inv, st = forward(
        lat, w_value, neighbours, edge_coef, grid_embed, gain_row, w_hidden, output_weight
    )
    r0 = permute(f[4:8], core_pairs())
    r1 = permute(jnp.concatenate([f[2:4], r0[2:4]]), ring_pairs("x", 0))
    r2 = permute(jnp.stack([f[1], r0[1], r1[1], r1[3]]), ring_pairs("x", 1))
    keep, send = slopes_of(valid_counts, f, r0, r1, r2, targets, var_weight[:, None], area[None, :])
    q2 = permute(send, ring_pairs("x", 1))
    q1 = permute(jnp.concatenate([keep[2:4], q2[2:4]]), ring_pairs("x", 0))
    q0 = permute(jnp.stack([keep[1], q2[1], q1[1], q1[3]]), core_pairs())
    parts = [keep, q2, q1, q0]
    pga, a1_keep, a1_send, go = upper(False, parts, output_weight, dg, hid, nta)
    pgb, a2_keep, a2_send = upper(True, parts, output_weight, dg, hid, ntb, go)
    b_keep, b_send, grad_latents = lower(pga, pgb, w_hidden, unit, inv, gain_row, st, lat, w_value)
    a1 = summed_shard(a1_keep, a1_send, ORDER_A1)
    a2 = summed_shard(a2_keep, a2_send, ORDER_A2)
    b = summed_shard(b_keep, b_send, ORDER_B)
    grad_hidden = jnp.concatenate([a1, a2[:, :1024]], axis=1)
    out = a2[:, 1024:].reshape(8, 2, 128).transpose(2, 1, 0).reshape(128, 16)[:100]
    return (b[:, :1024], b[:, 1024], grad_hidden, out, grad_latents[None])


def solution(mesh):
    in_specs = (
        P("member", "node", None),
        P("node", None),
        P(None, "node"),
        P(None, "node"),
        P(),
        P(),
        P(),
        P(),
        P(None, "node"),
        P(),
        P("node"),
        P(),
    )
    out_specs = (
        P(("member", "node"), None),
        P(("member", "node")),
        P(("member", "node"), None),
        P(None, ("member", "node")),
        P("member", "node", None),
    )
    return jax.shard_map(
        per_device, mesh=mesh, in_specs=in_specs, out_specs=out_specs, check_vma=False
    )
```

```python
import itertools

import jax
import jax.numpy as jnp
from jax import lax
from jax.experimental import pallas as pl
from jax.experimental.pallas import tpu as pltpu
from jax.sharding import PartitionSpec as P

BF = jnp.bfloat16
F32 = jnp.float32
kernel_width = 0.25
fair_alpha = 0.95
norm_eps = 1e-05
members = 8
GELU_C = 0.7978845608028654
VMEM = 56 * 1024 * 1024
CORE_AXES = ("x", "z", "y")
AXES = ("x", "core", "z", "y")


def flat(x, c, z, y):
    return ((x * 2 + c) * 4 + z) * 4 + y


def core_pairs():
    return [
        (flat(x, c, z, y), flat(x, 1 - c, z, y))
        for x, c, z, y in itertools.product(range(4), range(2), range(4), range(4))
    ]


def ring_pairs(axis):
    pairs = []
    for x, c, z, y in itertools.product(range(4), range(2), range(4), range(4)):
        to = {"x": x, "z": z, "y": y}
        to[axis] ^= (1, 3)[c]
        pairs.append((flat(x, c, z, y), flat(to["x"], c, to["z"], to["y"])))
    return pairs


def own_place():
    return {"x": lax.axis_index("x"), "c": lax.axis_index("core"), "z": lax.axis_index("z"), "y": lax.axis_index("y")}


def masks(core):
    first, second = 1 + 2 * core, 3 - 2 * core
    return (0, second, first, 2)


def x_pairs(position):
    pairs = []
    for x, c, z, y in itertools.product(range(4), range(2), range(4), range(4)):
        pairs.append((flat(x, c, z, y), flat(x ^ masks(c)[position], c, z, y)))
    return pairs


def dot(a, b, dims=((1,), (0,))):
    return lax.dot_general(a, b, (dims, ((), ())), preferred_element_type=F32)


def forward_kernel(
    lat_ref, wv_ref, nb_ref, cf_ref, emb_hbm, gain_ref, wh_ref, ow_ref,
    f0, f1, f2, f3, hid_ref, dg_ref, nrm_hbm, inv_ref, st_ref, lat_send,
    nrm, total, emb, sems,
):
    j = pl.program_id(0)
    nodes, points = st_ref.shape
    own = own_place()
    save = pltpu.make_async_copy(nrm, nrm_hbm, sems.at[1])

    @pl.when(j == 0)
    def _():
        load = pltpu.make_async_copy(emb_hbm, emb, sems.at[0])
        load.start()
        values = dot(lat_ref[...], wv_ref[...]).astype(BF)
        rows_of = lax.broadcasted_iota(jnp.int32, (nodes, 256), 0)
        for r in range(points // 256):
            rows = slice(256 * r, 256 * r + 256)
            st = jnp.zeros((nodes, 256), F32)
            for k in range(3):
                st = st + jnp.where(nb_ref[k : k + 1, rows] == rows_of, cf_ref[k : k + 1, rows], 0.0)
            st_ref[:, rows] = st.astype(BF)
        load.wait()
        for r in range(points // 256):
            rows = slice(256 * r, 256 * r + 256)
            summed = emb[rows, :].astype(F32) + dot(st_ref[:, rows], values, ((0,), (0,)))
            inv = lax.rsqrt(jnp.mean(summed * summed, axis=-1, keepdims=True) + norm_eps)
            inv_ref[rows, :] = inv
            nrm[rows, :] = (summed * inv * gain_ref[...]).astype(BF)
        save.start()
        total[...] = jnp.zeros_like(total)
        for x in range(4):
            columns = pl.ds(pl.multiple_of(x * 256 + (1 - own["c"]) * 128, 128), 128)
            lat_send[:, 128 * x : 128 * x + 128] = lat_ref[:, columns]

    step = 256
    for r in range(points // step):
        rows = slice(step * r, step * r + step)
        pre = dot(nrm[rows, :], wh_ref[...])
        square = pre * pre
        t = jnp.tanh(pre * (GELU_C + (GELU_C * 0.044715) * square))
        half = 0.5 * pre
        hid_ref[rows, :] = (half * t + half).astype(BF)
        slope = 0.5 + 0.5 * t + half * (1.0 - t * t) * (GELU_C + (3 * GELU_C * 0.044715) * square)
        dg_ref[rows, :] = slope.astype(BF)
    total[0:100, :] += dot(ow_ref[...], hid_ref[...], ((1,), (1,)))

    @pl.when(j == pl.num_programs(0) - 1)
    def _():
        for f, m in zip((f0, f1, f2, f3), masks(own["c"])):
            f[...] = total[:, pl.ds(pl.multiple_of((own["x"] ^ m) * 256, 256), 256)]
        save.wait()


def slopes_kernel(
    vc_ref, f0, f1, f2, f3, c0, c1, c2, c3, tg_ref, vw_ref, area_ref, s0, s1, s2, s3, held
):
    own = own_place()
    first = pl.multiple_of(own["x"] * 256, 256)
    spread = (1.0 - (1.0 - fair_alpha) / members) / (2.0 * members * (members - 1))
    held[:, 96:112, :] = jnp.zeros((4, 16, 256), F32)
    limit = vc_ref[own["z"] * 4 + own["y"]]
    for part in range(2):
        mine = pl.ds(pl.multiple_of(first + 128 * part, 128), 128)
        here = slice(128 * part, 128 * part + 128)
        place = first + 128 * part + lax.broadcasted_iota(jnp.int32, (1, 128), 1)
        live = jnp.where(place < limit, area_ref[:, mine], 0.0)
        for top in range(0, 100, 8):
            rows = slice(top, min(top + 8, 100))
            f = [field[rows, here] for field in (f0, f1, f2, f3, c0, c1, c2, c3)]
            sums = [jnp.zeros_like(f[0]) for _ in range(4)]
            for a in range(4):
                for b in range(a + 1, 8):
                    d = f[a] - f[b]
                    s = d * lax.rsqrt(d * d + kernel_width * kernel_width)
                    sums[a] = sums[a] + s
                    if b < 4:
                        sums[b] = sums[b] - s
            target = tg_ref[rows, mine]
            weight = vw_ref[rows, :] * live * 0.01
            for a in range(4):
                d = f[a] - target
                s = d * lax.rsqrt(d * d + kernel_width * kernel_width)
                held[a, rows, here] = weight * (s * (1.0 / members) - 2.0 * spread * sums[a])
    for a, s in enumerate((s0, s1, s2, s3)):
        s[...] = held[a].astype(BF)


def upper_kernel(
    s0, s1, s2, s3, ow_ref, dg_ref, hid_ref, nrm_ref,
    pg_ref, keep_ref, send_ref, go_keep, go_send,
    slopes, own_w, go, result,
):
    j = pl.program_id(0)
    points, wide = dg_ref.shape
    half = keep_ref.shape[0]
    own = own_place()

    @pl.when(j == 0)
    def _():
        for s, m in zip((s0, s1, s2, s3), masks(own["c"])):
            at = pl.ds(pl.multiple_of((own["x"] ^ m) * 256, 256), 256)
            slopes[0:112, at] = s[...]
        slopes[112:128, :] = jnp.zeros((16, points), BF)
        own_w[...] = jnp.zeros_like(own_w)

    own_w[0:100, :] = ow_ref[...]
    for r in range(points // 256):
        rows = slice(256 * r, 256 * r + 256)
        grad = dot(slopes[:, rows], own_w[...], ((0,), (0,)))
        pg_ref[rows, :] = (dg_ref[rows, :].astype(F32) * grad).astype(BF)
    result[...] = dot(nrm_ref[...], pg_ref[...], ((0,), (0,)))
    bit = jnp.where(j < 2, own["z"], own["x"]) & 1
    for k in range(2):
        columns = pl.ds(pl.multiple_of((bit ^ k) * 256, 256), 256)
        for ref, core in ((keep_ref, own["c"]), (send_ref, 1 - own["c"])):
            for x in range(4):
                rows = pl.ds(pl.multiple_of(x * 256 + core * 128, 128), 128)
                ref[128 * x : 128 * x + 128, 256 * k : 256 * k + 256] = result[rows, columns].astype(BF)
    go[:, pl.ds(pl.multiple_of(j * wide, wide), wide)] = dot(slopes[...], hid_ref[...])

    @pl.when(j == pl.num_programs(0) - 1)
    def _():
        for x in range(4):
            for ref, core in ((go_keep, own["c"]), (go_send, 1 - own["c"])):
                columns = pl.ds(pl.multiple_of(x * 512 + core * 256, 256), 256)
                ref[:, 256 * x : 256 * x + 256] = go[:, columns].astype(BF)


def lower_kernel(pg_ref, wh_ref, nrm_ref, inv_ref, gain_ref, st_ref, vg_ref, gain_sum, value_sum):
    j = pl.program_id(0)
    nodes = st_ref.shape[0]

    @pl.when(j == 0)
    def _():
        gain_sum[...] = jnp.zeros_like(gain_sum)
        value_sum[...] = jnp.zeros_like(value_sum)

    normed_grad = dot(pg_ref[...], wh_ref[...], ((1,), (1,)))
    normed = nrm_ref[...].astype(F32)
    product = normed_grad * normed
    gain_sum[...] += jnp.sum(product, axis=0, keepdims=True)
    mean = jnp.mean(product, axis=-1, keepdims=True)
    gain = gain_ref[...]
    summed_grad = inv_ref[...] * (normed_grad * gain - normed * (1.0 / gain) * mean)
    value_sum[...] += dot(st_ref[...], summed_grad.astype(BF))

    @pl.when(j == pl.num_programs(0) - 1)
    def _():
        vg_ref[0:nodes, :] = value_sum[...].astype(BF)
        vg_ref[nodes:, :] = jnp.broadcast_to(gain_sum[...] / gain_ref[...], (16, gain.shape[1])).astype(BF)


def latents_kernel(vg_ref, wv_ref, gl_ref):
    gl_ref[...] = dot(vg_ref[0 : gl_ref.shape[0], :], wv_ref[...], ((1,), (1,))).astype(BF)


def value_kernel(
    lat_ref, lat_recv, vg_ref, vg_recv, go_keep, go_recv, b_ref, own_lat, gain_turned
):
    nodes, width = lat_ref.shape
    core = lax.axis_index("core")
    gain = vg_ref[nodes:, :].astype(F32)[0:8] + vg_recv[nodes:, :].astype(F32)[0:8]
    gain = jnp.broadcast_to(gain[0:1], (128, width)).T
    gain_turned[...] = gain
    for x in range(4):
        columns = pl.ds(pl.multiple_of(x * 256 + core * 128, 128), 128)
        own_lat[:, 128 * x : 128 * x + 128] = lat_ref[:, columns]
    value = dot(own_lat[...], vg_ref[0:nodes, :], ((0,), (0,)))
    value = value + dot(lat_recv[...], vg_recv[0:nodes, :], ((0,), (0,)))
    b_ref[:, 0:width] = value.astype(BF)
    out = (go_keep[...].astype(F32) + go_recv[...].astype(F32)).T.reshape(64, 2, 8, 128)
    for k in range(2):
        b_ref[:, width + 128 * k : width + 128 * k + 128] = out[:, k].reshape(512, 128).astype(BF)
    for x in range(4):
        rows = pl.ds(pl.multiple_of(x * 256 + core * 128, 128), 128)
        b_ref[128 * x : 128 * x + 128, width + 256 :] = gain_turned[rows, :].astype(BF)


def whole(shape):
    return pl.BlockSpec(shape, lambda j: (0,) * len(shape))


def params():
    return pltpu.CompilerParams(vmem_limit_bytes=VMEM, dimension_semantics=("arbitrary",))


def cost(flops, moved):
    return pl.CostEstimate(flops=flops, bytes_accessed=moved, transcendentals=0)


def like(shape, dtype=BF):
    return jax.ShapeDtypeStruct(shape, dtype)


def forward(lat, wv, nb, cf, emb, gain, wh, ow):
    nodes, width = lat.shape
    points = emb.shape[0]
    hidden = wh.shape[1]
    wide = 512
    tile = pl.BlockSpec((points, wide), lambda j: (0, j))
    raw = pl.BlockSpec(memory_space=pl.ANY)
    return pl.pallas_call(
        forward_kernel,
        grid=(hidden // wide,),
        in_specs=[
            whole(lat.shape), whole(wv.shape), whole(nb.shape), whole(cf.shape), raw, whole(gain.shape),
            pl.BlockSpec((width, wide), lambda j: (0, j)),
            pl.BlockSpec((ow.shape[0], wide), lambda j: (0, j)),
        ],
        out_specs=[whole((104, 256))] * 4
        + [tile, tile, raw, whole((points, 1)), whole((nodes, points)), whole((nodes, width // 2))],
        out_shape=[like((104, 256), F32)] * 4
        + [
            like((points, hidden)), like((points, hidden)), like((points, width)),
            like((points, 1), F32), like((nodes, points)), like((nodes, width // 2)),
        ],
        scratch_shapes=[
            pltpu.VMEM((points, width), BF),
            pltpu.VMEM((104, points), F32),
            pltpu.VMEM((points, width), BF),
            pltpu.SemaphoreType.DMA((2,)),
        ],
        compiler_params=params(),
        cost_estimate=cost(6_400_000_000, 30_000_000),
        name="forward",
    )(lat, wv, nb, cf, emb, gain, wh, ow)


def in_vmem(kernel, name, out_shape, scratch, estimate, *args, scalars=0):
    vm = pl.BlockSpec(memory_space=pltpu.VMEM)
    many = isinstance(out_shape, list)
    return pl.pallas_call(
        kernel,
        in_specs=[pl.BlockSpec(memory_space=pltpu.SMEM)] * scalars + [vm] * (len(args) - scalars),
        out_specs=[vm] * len(out_shape) if many else vm,
        out_shape=out_shape,
        scratch_shapes=scratch,
        compiler_params=pltpu.CompilerParams(vmem_limit_bytes=VMEM),
        cost_estimate=estimate,
        name=name,
    )(*args)


def upper(parts, ow, dg, hid, nrm):
    points, hidden = dg.shape
    width = nrm.shape[1]
    wide = 512
    col = lambda n: pl.BlockSpec((n, wide), lambda j: (0, j))

    def place(j):
        bit = jnp.where(j < 2, lax.axis_index("x"), lax.axis_index("z")) & 1
        return (0, j ^ bit)

    piece = pl.BlockSpec((width // 2, wide), place)
    return pl.pallas_call(
        upper_kernel,
        grid=(hidden // wide,),
        in_specs=[whole(p.shape) for p in parts] + [col(ow.shape[0]), col(points), col(points), whole(nrm.shape)],
        out_specs=[col(points), piece, piece, whole((128, hidden // 2)), whole((128, hidden // 2))],
        out_shape=[
            like((points, hidden)), like((width // 2, hidden)), like((width // 2, hidden)),
            like((128, hidden // 2)), like((128, hidden // 2)),
        ],
        scratch_shapes=[
            pltpu.VMEM((128, points), BF), pltpu.VMEM((128, wide), BF),
            pltpu.VMEM((128, hidden), F32), pltpu.VMEM((width, wide), F32),
        ],
        compiler_params=params(),
        cost_estimate=cost(5_400_000_000, 24_000_000),
        name="upper",
    )(*parts, ow, dg, hid, nrm)


def lower(pg, wh, nrm, inv, gain, st):
    points, width = nrm.shape
    nodes = st.shape[0]
    step = 256
    rows = lambda n: pl.BlockSpec((step, n), lambda j: (j, 0))
    return pl.pallas_call(
        lower_kernel,
        grid=(points // step,),
        in_specs=[
            rows(pg.shape[1]), whole(wh.shape), rows(width), rows(1), whole(gain.shape),
            pl.BlockSpec((nodes, step), lambda j: (0, j)),
        ],
        out_specs=whole((nodes + 16, width)),
        out_shape=like((nodes + 16, width)),
        scratch_shapes=[pltpu.VMEM((1, width), F32), pltpu.VMEM((nodes, width), F32)],
        compiler_params=params(),
        cost_estimate=cost(5_100_000_000, 16_000_000),
        name="lower",
    )(pg, wh, nrm, inv, gain, st)


def permute(value, pairs):
    return lax.ppermute(value, AXES, pairs)


def total_of(parts, tile):
    return sum(part[:, 512 * tile : 512 * tile + 512].astype(F32) for part in parts)


def per_device(
    latents, grid_embed, neighbours, edge_coef, w_value, gain, w_hidden, output_weight,
    targets, var_weight, area, valid_counts,
):
    lat = latents[0]
    gain_row = gain[None, :]
    f0, f1, f2, f3, hid, dg, nrm, inv, st, lat_send = forward(
        lat, w_value, neighbours, edge_coef, grid_embed, gain_row, w_hidden, output_weight
    )
    core = core_pairs()
    r3 = permute(f3, x_pairs(3))
    r1 = permute(f1, x_pairs(1))
    r2 = permute(f2, x_pairs(2))
    c0, c1, c2, c3 = (permute(f, core) for f in (f0, r1, r2, r3))
    s0, s1, s2, s3 = in_vmem(
        slopes_kernel, "slopes", [like((112, 256))] * 4, [pltpu.VMEM((4, 112, 256), F32)],
        cost(20_000_000, 3_000_000),
        valid_counts, f0, r1, r2, r3, c0, c1, c2, c3, targets, var_weight[:, None], area[None, :], scalars=1,
    )
    q3 = permute(s3, x_pairs(3))
    q1 = permute(s1, x_pairs(1))
    q2 = permute(s2, x_pairs(2))
    lat_recv = permute(lat_send, core)
    pg, a_keep, a_send, go_keep, go_send = upper([s0, q1, q2, q3], output_weight, dg, hid, nrm)
    a = [a_keep, permute(a_send, core)]
    go_recv = permute(go_send, core)
    vg = lower(pg, w_hidden, nrm, inv, gain_row, st)
    width = vg.shape[1]
    first = [permute(total_of(a, k).astype(BF), ring_pairs(axis)) for k, axis in ((1, "x"), (3, "z"))]
    vg_recv = permute(vg, core)
    grad_latents = in_vmem(latents_kernel, "grad_latents", like(lat.shape), [], cost(800_000_000, 4_000_000), vg, w_value)
    b = in_vmem(
        value_kernel, "grad_value", like((width // 2, width + 384)),
        [pltpu.VMEM((lat.shape[0], width // 2), BF), pltpu.VMEM((width, 128), F32)],
        cost(800_000_000, 6_000_000),
        lat, lat_recv, vg, vg_recv, go_keep, go_recv,
    )
    quarters = []
    for k, axis, half in ((0, "z", first[0]), (2, "x", first[1])):
        kept = total_of(a, k) + half.astype(F32)
        quarters.append(kept[:, :256] + permute(kept[:, 256:].astype(BF), ring_pairs(axis)).astype(F32))
    mine = jnp.concatenate([quarters[0].astype(BF), quarters[1].astype(BF), b], axis=1)
    sent = mine.reshape(64, 8, mine.shape[1])
    met = lax.all_to_all(sent, CORE_AXES, 0, 0, tiled=True)
    met = met.reshape(2, 2, 2, 2, 4, 8, met.shape[2])
    a_sum = jnp.sum(met[..., :512].astype(F32), axis=(0, 2, 4))
    b_sum = jnp.sum(met[..., 512:].astype(F32), axis=(0, 1, 2, 3, 4))
    a_first = a_sum[..., :256].transpose(2, 0, 1, 3).reshape(8, 1024)
    a_second = a_sum[..., 256:].transpose(2, 1, 0, 3).reshape(8, 1024)
    grad_hidden = jnp.concatenate([a_first, a_second], axis=1)
    out = b_sum[:, width : width + 256].reshape(8, 2, 128).transpose(2, 1, 0).reshape(128, 16)[:100]
    return (b_sum[:, :width], b_sum[:, width + 256], grad_hidden, out, grad_latents[None])


def solution(mesh):
    mesh = jax.sharding.Mesh(mesh.devices.reshape(4, 2, 4, 4), AXES)
    member, node = ("x", "core"), ("z", "y")
    in_specs = (
        P(member, node, None),
        P(node, None),
        P(None, node),
        P(None, node),
        P(),
        P(),
        P(),
        P(),
        P(None, node),
        P(),
        P(node),
        P(),
    )
    out_specs = (
        P(AXES, None),
        P(AXES),
        P(AXES, None),
        P(None, AXES),
        P(member, node, None),
    )
    return jax.shard_map(
        per_device, mesh=mesh, in_specs=in_specs, out_specs=out_specs, check_vma=False
    )
```

```python
import itertools

import jax
import jax.numpy as jnp
from jax import lax
from jax.experimental import pallas as pl
from jax.experimental.pallas import tpu as pltpu
from jax.sharding import PartitionSpec as P

BF = jnp.bfloat16
F32 = jnp.float32
kernel_width = 0.25
fair_alpha = 0.95
norm_eps = 1e-05
members = 8
GELU_C = 0.7978845608028654
MIB = 1024 * 1024
CORE_AXES = ("x", "z", "y")
AXES = ("x", "core", "z", "y")


def flat(x, c, z, y):
    return ((x * 2 + c) * 4 + z) * 4 + y


def core_pairs():
    return [
        (flat(x, c, z, y), flat(x, 1 - c, z, y))
        for x, c, z, y in itertools.product(range(4), range(2), range(4), range(4))
    ]


def ring_pairs(axis):
    pairs = []
    for x, c, z, y in itertools.product(range(4), range(2), range(4), range(4)):
        to = {"x": x, "z": z, "y": y}
        to[axis] ^= (1, 3)[c]
        pairs.append((flat(x, c, z, y), flat(to["x"], c, to["z"], to["y"])))
    return pairs


def own_place():
    return {"x": lax.axis_index("x"), "c": lax.axis_index("core"), "z": lax.axis_index("z"), "y": lax.axis_index("y")}


def masks(core):
    first, second = 1 + 2 * core, 3 - 2 * core
    return (0, second, first, 2)


def x_pairs(position):
    pairs = []
    for x, c, z, y in itertools.product(range(4), range(2), range(4), range(4)):
        pairs.append((flat(x, c, z, y), flat(x ^ masks(c)[position], c, z, y)))
    return pairs


def dot(a, b, dims=((1,), (0,))):
    return lax.dot_general(a, b, (dims, ((), ())), preferred_element_type=F32)


def forward_kernel(
    lat_hbm, wv_hbm, nb_hbm, cf_hbm, emb_hbm, gain_hbm, wh_hbm, ow_hbm,
    f0, f1, f2, f3, hid_ref, dg_ref, nrm, inv_ref, st_ref, lat_send,
    total, lat, wv, emb, wh, ow, nb_ref, cf_ref, gain_ref, sems,
):
    nodes, points = st_ref.shape
    hidden = wh.shape[1]
    wide = 512
    own = own_place()
    pairs = [(lat_hbm, lat), (wv_hbm, wv), (emb_hbm, emb)]
    for first in range(0, hidden, wide):
        pairs.append((wh_hbm.at[:, first : first + wide], wh.at[:, first : first + wide]))
    pairs += [(ow_hbm, ow), (nb_hbm, nb_ref), (cf_hbm, cf_ref), (gain_hbm, gain_ref)]
    small = len(pairs) - 4
    copies = [pltpu.make_async_copy(source, target, sems.at[k]) for k, (source, target) in enumerate(pairs)]
    for k in (*range(small + 1, small + 4), *range(small + 1)):
        copies[k].start()
    for copy in copies[small + 1 :]:
        copy.wait()
    rows_of = lax.broadcasted_iota(jnp.int32, (nodes, 256), 0)
    for r in range(points // 256):
        rows = slice(256 * r, 256 * r + 256)
        st = jnp.zeros((nodes, 256), F32)
        for k in range(3):
            st = st + jnp.where(nb_ref[k : k + 1, rows] == rows_of, cf_ref[k : k + 1, rows], 0.0)
        st_ref[:, rows] = st.astype(BF)
    total[...] = jnp.zeros_like(total)
    copies[0].wait()
    copies[1].wait()
    values = dot(lat[...], wv[...]).astype(BF)
    for x in range(4):
        columns = pl.ds(pl.multiple_of(x * 256 + (1 - own["c"]) * 128, 128), 128)
        lat_send[:, 128 * x : 128 * x + 128] = lat[:, columns]
    copies[2].wait()
    for r in range(points // 256):
        rows = slice(256 * r, 256 * r + 256)
        summed = emb[rows, :].astype(F32) + dot(st_ref[:, rows], values, ((0,), (0,)))
        inv = lax.rsqrt(jnp.mean(summed * summed, axis=-1, keepdims=True) + norm_eps)
        inv_ref[rows, :] = inv
        nrm[rows, :] = (summed * inv * gain_ref[...]).astype(BF)
    copies[small].wait()
    for tile in range(hidden // wide):
        here = slice(wide * tile, wide * tile + wide)
        copies[3 + tile].wait()
        for r in range(points // 256):
            rows = slice(256 * r, 256 * r + 256)
            pre = dot(nrm[rows, :], wh[:, here])
            square = pre * pre
            t = jnp.tanh(pre * (GELU_C + (GELU_C * 0.044715) * square))
            cdf = 0.5 + 0.5 * t
            hid_ref[rows, here] = (pre * cdf).astype(BF)
            inner = pre * (GELU_C + (3 * GELU_C * 0.044715) * square)
            dg_ref[rows, here] = (cdf * (1.0 + (1.0 - t) * inner)).astype(BF)
        total[0:100, :] += dot(ow[:, here], hid_ref[:, here], ((1,), (1,)))
    for f, m in zip((f0, f1, f2, f3), masks(own["c"])):
        f[...] = total[:, pl.ds(pl.multiple_of((own["x"] ^ m) * 256, 256), 256)]


def slopes_kernel(
    vc_ref, f0, f1, f2, f3, c0, c1, c2, c3, tg_ref, vw_ref, area_ref, s0, s1, s2, s3, held
):
    own = own_place()
    first = pl.multiple_of(own["x"] * 256, 256)
    spread = (1.0 - (1.0 - fair_alpha) / members) / (2.0 * members * (members - 1))
    held[:, 96:112, :] = jnp.zeros((4, 16, 256), F32)
    limit = vc_ref[own["z"] * 4 + own["y"]]
    across = lax.broadcasted_iota(jnp.int32, (104, 100), 1)
    down = lax.broadcasted_iota(jnp.int32, (104, 100), 0)
    weights = jnp.sum(jnp.where(across == down, vw_ref[...], 0.0), axis=1, keepdims=True) * 0.01
    for part in range(2):
        mine = pl.ds(pl.multiple_of(first + 128 * part, 128), 128)
        here = slice(128 * part, 128 * part + 128)
        place = first + 128 * part + lax.broadcasted_iota(jnp.int32, (1, 128), 1)
        live = jnp.where(place < limit, area_ref[:, mine], 0.0)
        for top in range(0, 100, 8):
            rows = slice(top, min(top + 8, 100))
            f = [field[rows, here] for field in (f0, f1, f2, f3, c0, c1, c2, c3)]
            sums = [jnp.zeros_like(f[0]) for _ in range(4)]
            for a in range(4):
                for b in range(a + 1, 8):
                    d = f[a] - f[b]
                    s = d * lax.rsqrt(d * d + kernel_width * kernel_width)
                    sums[a] = sums[a] + s
                    if b < 4:
                        sums[b] = sums[b] - s
            target = tg_ref[rows, mine]
            weight = weights[rows, :] * live
            for a in range(4):
                d = f[a] - target
                s = d * lax.rsqrt(d * d + kernel_width * kernel_width)
                held[a, rows, here] = weight * (s * (1.0 / members) - 2.0 * spread * sums[a])
    for a, s in enumerate((s0, s1, s2, s3)):
        s[...] = held[a].astype(BF)


def upper_kernel(
    axis, s0, s1, s2, s3, ow_ref, dg_ref, nrm_ref, *rest
):
    if axis == "z":
        hid_ref, pg_ref, keep_ref, send_ref, go_keep, go_send, slopes, own_w, result, go = rest
    else:
        pg_ref, keep_ref, send_ref, slopes, own_w, result = rest
    points = nrm_ref.shape[0]
    offset = 1024 if axis == "z" else 0
    own = own_place()
    for s, m in zip((s0, s1, s2, s3), masks(own["c"])):
        at = pl.ds(pl.multiple_of((own["x"] ^ m) * 256, 256), 256)
        slopes[0:112, at] = s[...]
    slopes[112:128, :] = jnp.zeros((16, points), BF)
    own_w[96:128, :] = jnp.zeros((32, 1024), BF)
    own_w[0:100, :] = ow_ref[:, offset : offset + 1024]
    for r in range(points // 256):
        rows = slice(256 * r, 256 * r + 256)
        grad = dot(slopes[:, rows], own_w[...], ((0,), (0,)))
        pg_ref[rows, :] = (dg_ref[rows, offset : offset + 1024].astype(F32) * grad).astype(BF)
    for tile in range(2):
        result[...] = dot(nrm_ref[...], pg_ref[:, 512 * tile : 512 * tile + 512], ((0,), (0,)))
        columns = pl.ds(pl.multiple_of((tile ^ (own[axis] & 1)) * 512, 512), 512)
        for ref, core in ((keep_ref, own["c"]), (send_ref, 1 - own["c"])):
            for x in range(4):
                rows = pl.ds(pl.multiple_of(x * 256 + core * 128, 128), 128)
                ref[128 * x : 128 * x + 128, columns] = result[rows, :].astype(BF)
    if axis == "z":
        go[...] = dot(slopes[...], hid_ref[...])
        for x in range(4):
            for ref, core in ((go_keep, own["c"]), (go_send, 1 - own["c"])):
                columns = pl.ds(pl.multiple_of(x * 512 + core * 256, 256), 256)
                ref[:, 256 * x : 256 * x + 256] = go[:, columns].astype(BF)


def lower_kernel(pga_ref, pgb_ref, wh_ref, nrm_ref, inv_ref, gain_ref, st_ref, top_ref, rest_ref, value_sum):
    nodes, points = st_ref.shape
    top = top_ref.shape[0]
    gain = gain_ref[...]
    over_gain = 1.0 / gain
    gain_sum = jnp.zeros_like(gain)
    for r in range(points // 256):
        rows = slice(256 * r, 256 * r + 256)
        normed_grad = dot(pga_ref[rows, :], wh_ref[:, 0:1024], ((1,), (1,)))
        normed_grad = normed_grad + dot(pgb_ref[rows, :], wh_ref[:, 1024:2048], ((1,), (1,)))
        normed = nrm_ref[rows, :].astype(F32)
        product = normed_grad * normed
        gain_sum = gain_sum + jnp.sum(product, axis=0, keepdims=True)
        mean = jnp.mean(product, axis=-1, keepdims=True)
        summed_grad = inv_ref[rows, :] * (normed_grad * gain - normed * over_gain * mean)
        part = dot(st_ref[:, rows], summed_grad.astype(BF))
        value_sum[...] = part if r == 0 else value_sum[...] + part
    top_ref[...] = value_sum[0:top, :].astype(BF)
    rest_ref[0 : nodes - top, :] = value_sum[top:nodes, :].astype(BF)
    rest_ref[nodes - top :, :] = jnp.broadcast_to(gain_sum * over_gain, (16, gain.shape[1])).astype(BF)


def latents_kernel(top_ref, rest_ref, wv_ref, gl_ref):
    top = top_ref.shape[0]
    gl_ref[0:top, :] = dot(top_ref[...], wv_ref[...], ((1,), (1,))).astype(BF)
    gl_ref[top:, :] = dot(rest_ref[0 : gl_ref.shape[0] - top, :], wv_ref[...], ((1,), (1,))).astype(BF)


def value_kernel(
    lat_ref, lat_recv, top_ref, rest_ref, top_recv, rest_recv, go_keep, go_recv, first_ref, second_ref,
    out_hbm, own_lat, gain_turned, block, sems,
):
    nodes, width = lat_ref.shape
    variables = 100
    core = lax.axis_index("core")
    copies = [
        pltpu.make_async_copy(first_ref, out_hbm.at[:, 0:512], sems.at[0]),
        pltpu.make_async_copy(second_ref, out_hbm.at[:, 512:1024], sems.at[1]),
        pltpu.make_async_copy(block, out_hbm.at[:, 1024:], sems.at[2]),
    ]
    copies[0].start()
    copies[1].start()
    top = top_ref.shape[0]
    bottom = nodes - top
    gain = rest_ref[bottom:, :].astype(F32)[0:8] + rest_recv[bottom:, :].astype(F32)[0:8]
    gain_turned[...] = jnp.broadcast_to(gain[0:1], (128, width)).T
    for x in range(4):
        columns = pl.ds(pl.multiple_of(x * 256 + core * 128, 128), 128)
        own_lat[:, 128 * x : 128 * x + 128] = lat_ref[:, columns]
    value = dot(own_lat[0:top, :], top_ref[...], ((0,), (0,)))
    value = value + dot(own_lat[top:, :], rest_ref[0:bottom, :], ((0,), (0,)))
    value = value + dot(lat_recv[0:top, :], top_recv[...], ((0,), (0,)))
    value = value + dot(lat_recv[top:, :], rest_recv[0:bottom, :], ((0,), (0,)))
    block[:, 0:width] = value.astype(BF)
    out = (go_keep[...].astype(F32) + go_recv[...].astype(F32)).T.reshape(64, 2, 8, 128)
    lane = lax.broadcasted_iota(jnp.int32, (128, 128), 1)
    for x in range(4):
        rows = slice(128 * x, 128 * x + 128)
        own_gain = gain_turned[pl.ds(pl.multiple_of(x * 256 + core * 128, 128), 128), :]
        first = out[16 * x : 16 * x + 16, 0].reshape(128, 128)
        block[rows, width : width + 128] = jnp.where(lane == variables, own_gain, first).astype(BF)
        block[rows, width + 128 :] = out[16 * x : 16 * x + 16, 1].reshape(128, 128).astype(BF)
    copies[2].start()
    for copy in copies:
        copy.wait()


def final_kernel(met_ref, value_ref, gain_ref, hidden_ref, out_ref):
    width = value_ref.shape[1]
    first, second = [None, None], [None, None]
    rest = None
    for x in range(4):
        for z in range(4):
            for y in range(4):
                block = met_ref[x * 16 + z * 4 + y].astype(F32)
                for sums, k, columns in ((first, x & 1, slice(0, 512)), (second, z & 1, slice(512, 1024))):
                    sums[k] = block[:, columns] if sums[k] is None else sums[k] + block[:, columns]
                rest = block[:, 1024:] if rest is None else rest + block[:, 1024:]
    for k, part in enumerate(first + second):
        hidden_ref[:, 512 * k : 512 * k + 512] = part
    value_ref[...] = rest[:, :width]
    variables = out_ref.shape[1]
    out_ref[0:8, :] = rest[:, width : width + variables]
    out_ref[8:16, :] = rest[:, width + 128 : width + 128 + variables]
    gain_ref[...] = rest[:, width : width + 128].T[variables : variables + 1]


def cost(flops, moved):
    return pl.CostEstimate(flops=flops, bytes_accessed=moved, transcendentals=0)


def like(shape, dtype=BF):
    return jax.ShapeDtypeStruct(shape, dtype)


def held(*arrays):
    return [pltpu.with_memory_space_constraint(array, pltpu.VMEM) for array in arrays]


def forward(lat, wv, nb, cf, emb, gain, wh, ow):
    nodes, width = lat.shape
    points = emb.shape[0]
    hidden = wh.shape[1]
    vm = pl.BlockSpec(memory_space=pltpu.VMEM)
    raw = pl.BlockSpec(memory_space=pl.ANY)
    args = [pltpu.with_memory_space_constraint(array, pltpu.HBM) for array in (lat, wv, nb, cf, emb, gain, wh, ow)]
    return pl.pallas_call(
        forward_kernel,
        in_specs=[raw] * 8,
        out_specs=[vm] * 10,
        out_shape=[like((104, 256), F32)] * 4
        + [
            pltpu.VMEM((points, hidden), BF), pltpu.VMEM((points, hidden), BF), pltpu.VMEM((points, width), BF),
            pltpu.VMEM((points, 1), F32), pltpu.VMEM((nodes, points), BF), like((nodes, width // 2)),
        ],
        scratch_shapes=[
            pltpu.VMEM((104, points), F32), pltpu.VMEM((nodes, width), BF), pltpu.VMEM((width, width), BF),
            pltpu.VMEM((points, width), BF), pltpu.VMEM((width, hidden), BF), pltpu.VMEM(ow.shape, BF),
            pltpu.VMEM(nb.shape, jnp.int32), pltpu.VMEM(cf.shape, F32), pltpu.VMEM(gain.shape, F32),
            pltpu.SemaphoreType.DMA((7 + hidden // 512,)),
        ],
        compiler_params=pltpu.CompilerParams(vmem_limit_bytes=24 * MIB),
        cost_estimate=cost(6_400_000_000, 12_000_000),
        name="forward",
    )(*args)


def in_vmem(kernel, name, out_shape, scratch, estimate, limit, *args, scalars=0, in_hbm=False):
    vm = pl.BlockSpec(memory_space=pltpu.VMEM)
    many = isinstance(out_shape, list)
    return pl.pallas_call(
        kernel,
        in_specs=[pl.BlockSpec(memory_space=pltpu.SMEM)] * scalars + [vm] * (len(args) - scalars),
        out_specs=[vm] * len(out_shape) if many else pl.BlockSpec(memory_space=pl.ANY) if in_hbm else vm,
        out_shape=out_shape,
        scratch_shapes=scratch,
        compiler_params=pltpu.CompilerParams(vmem_limit_bytes=limit * MIB),
        cost_estimate=estimate,
        name=name,
    )(*args)


def upper(axis, parts, ow, dg, nrm, *hid):
    points, width = nrm.shape
    half = like((width // 2, 1024))
    out_shape = [pltpu.VMEM((points, 1024), BF), half, half]
    scratch = [pltpu.VMEM((128, points), BF), pltpu.VMEM((128, 1024), BF), pltpu.VMEM((width, 512), F32)]
    if axis == "z":
        out_shape += [like((128, 1024)), like((128, 1024))]
        scratch.append(pltpu.VMEM((128, 2048), F32))
    return in_vmem(
        lambda *refs: upper_kernel(axis, *refs), "upper_" + axis, out_shape, scratch, cost(2_700_000_000, 2_000_000), 20,
        *parts, ow, *held(dg, nrm, *hid),
    )


def permute(value, pairs):
    return lax.ppermute(value, AXES, pairs)


def total_of(parts, tile):
    return sum(part[:, 512 * tile : 512 * tile + 512].astype(F32) for part in parts)


def per_device(
    latents, grid_embed, neighbours, edge_coef, w_value, gain, w_hidden, output_weight,
    targets, var_weight, area, valid_counts,
):
    lat = latents[0]
    gain_row = gain[None, :]
    f0, f1, f2, f3, hid, dg, nrm, inv, st, lat_send = forward(
        lat, w_value, neighbours, edge_coef, grid_embed, gain_row, w_hidden, output_weight
    )
    core = core_pairs()
    r3 = permute(f3, x_pairs(3))
    r1 = permute(f1, x_pairs(1))
    r2 = permute(f2, x_pairs(2))
    c0, c1, c2, c3 = (permute(f, core) for f in (f0, r1, r2, r3))
    s0, s1, s2, s3 = in_vmem(
        slopes_kernel, "slopes", [like((112, 256))] * 4, [pltpu.VMEM((4, 112, 256), F32)],
        cost(20_000_000, 3_000_000), 16,
        valid_counts, f0, r1, r2, r3, c0, c1, c2, c3, targets, var_weight[None, :], area[None, :], scalars=1,
    )
    q3 = permute(s3, x_pairs(3))
    q1 = permute(s1, x_pairs(1))
    q2 = permute(s2, x_pairs(2))
    lat_recv = permute(lat_send, core)
    parts = [s0, q1, q2, q3]
    pga, *first = upper("x", parts, output_weight, dg, nrm)
    first[1] = permute(first[1], core)
    pgb, keep, send, go_keep, go_send = upper("z", parts, output_weight, dg, nrm, hid)
    second = [keep, permute(send, core)]
    go_recv = permute(go_send, core)
    sent, pgb = lax.optimization_barrier((total_of(first, 1).astype(BF), pgb))
    first.append(permute(sent, ring_pairs("x")))
    nodes, width = lat.shape
    top, rest = in_vmem(
        lower_kernel, "lower", [like((192, width)), like((nodes - 192 + 16, width))], [pltpu.VMEM((nodes, width), F32)],
        cost(5_100_000_000, 8_000_000), 24,
        *held(pga, pgb), w_hidden, *held(nrm, inv), gain_row, *held(st),
    )
    second.append(permute(total_of(second, 1).astype(BF), ring_pairs("z")))
    halves = [total_of(part, 0).astype(BF) for part in (first, second)]
    *halves, top, rest = lax.optimization_barrier((*halves, top, rest))
    top_recv, rest_recv = permute(top, core), permute(rest, core)
    grad_latents = in_vmem(
        latents_kernel, "grad_latents", like(lat.shape), [], cost(800_000_000, 4_000_000), 16, top, rest, w_value
    )
    mine = in_vmem(
        value_kernel, "grad_value", pltpu.HBM((width // 2, 1024 + width + 256), BF),
        [
            pltpu.VMEM((nodes, width // 2), BF), pltpu.VMEM((width, 128), F32),
            pltpu.VMEM((width // 2, width + 256), BF), pltpu.SemaphoreType.DMA((3,)),
        ],
        cost(800_000_000, 6_000_000), 16,
        lat, lat_recv, top, rest, top_recv, rest_recv, go_keep, go_recv, *halves, in_hbm=True,
    )
    sent = mine.reshape(64, 8, mine.shape[1])
    met = lax.all_to_all(sent, CORE_AXES, 0, 0, tiled=True)
    grad_value, grad_gain, grad_hidden, grad_out = in_vmem(
        final_kernel, "final", [like((8, width), F32), like((1, 8), F32), like((8, 2048), F32), like((16, 100), F32)],
        [], cost(2_000_000, 2_600_000), 16, met,
    )
    return (grad_value, grad_gain.reshape(8), grad_hidden, grad_out.T, grad_latents[None])


def solution(mesh):
    mesh = jax.sharding.Mesh(mesh.devices.reshape(4, 2, 4, 4), AXES)
    member, node = ("x", "core"), ("z", "y")
    in_specs = (
        P(member, node, None),
        P(node, None),
        P(None, node),
        P(None, node),
        P(),
        P(),
        P(),
        P(),
        P(None, node),
        P(),
        P(node),
        P(),
    )
    out_specs = (
        P(AXES, None),
        P(AXES),
        P(AXES, None),
        P(None, AXES),
        P(member, node, None),
    )
    return jax.shard_map(
        per_device, mesh=mesh, in_specs=in_specs, out_specs=out_specs, check_vma=False
    )
```

```python
import itertools

import jax
import jax.numpy as jnp
from jax import lax
from jax.experimental import pallas as pl
from jax.experimental.pallas import tpu as pltpu
from jax.sharding import PartitionSpec as P

BF = jnp.bfloat16
F32 = jnp.float32
kernel_width = 0.25
fair_alpha = 0.95
norm_eps = 1e-05
members = 8
GELU_C = 0.7978845608028654
MIB = 1024 * 1024
CORE_AXES = ("x", "z", "y")
AXES = ("x", "core", "z", "y")


def flat(x, c, z, y):
    return ((x * 2 + c) * 4 + z) * 4 + y


def core_pairs():
    return [
        (flat(x, c, z, y), flat(x, 1 - c, z, y))
        for x, c, z, y in itertools.product(range(4), range(2), range(4), range(4))
    ]


def ring_pairs(axis):
    pairs = []
    for x, c, z, y in itertools.product(range(4), range(2), range(4), range(4)):
        to = {"x": x, "z": z, "y": y}
        to[axis] ^= (1, 3)[c]
        pairs.append((flat(x, c, z, y), flat(to["x"], c, to["z"], to["y"])))
    return pairs


def own_place():
    return {"x": lax.axis_index("x"), "c": lax.axis_index("core"), "z": lax.axis_index("z"), "y": lax.axis_index("y")}


def masks(core):
    first, second = 1 + 2 * core, 3 - 2 * core
    return (0, second, first, 2)


def x_pairs(position):
    pairs = []
    for x, c, z, y in itertools.product(range(4), range(2), range(4), range(4)):
        pairs.append((flat(x, c, z, y), flat(x ^ masks(c)[position], c, z, y)))
    return pairs


def dot(a, b, dims=((1,), (0,))):
    return lax.dot_general(a, b, (dims, ((), ())), preferred_element_type=F32)


def cdf_of(pre):
    return 0.5 + 0.5 * jnp.tanh(pre * (GELU_C + (GELU_C * 0.044715) * (pre * pre)))


def gelu_slope_kernel(pre_ref, dg_ref):
    def body(q, carry):
        for part in range(4):
            rows = pl.ds(pl.multiple_of(q * 64 + 16 * part, 16), 16)
            pre = pre_ref[rows, :].astype(F32)
            square = pre * pre
            t = jnp.tanh(pre * (GELU_C + (GELU_C * 0.044715) * square))
            inner = pre * (GELU_C + (3 * GELU_C * 0.044715) * square)
            dg_ref[rows, :] = ((0.5 + 0.5 * t) * (1.0 + (1.0 - t) * inner)).astype(BF)
        return carry

    lax.fori_loop(0, pre_ref.shape[0] // 64, body, 0)


def forward_kernel(
    lat_hbm, wv_hbm, nb_hbm, cf_hbm, emb_hbm, gain_hbm, wh_hbm, ow_hbm,
    f0, f1, f2, f3, hid_ref, pre_ref, nrm, inv_ref, st_ref, lat_send,
    total, lat, wv, emb, wh, ow, nb_ref, cf_ref, gain_ref, sems,
):
    nodes, points = st_ref.shape
    hidden = wh.shape[1]
    wide = 512
    own = own_place()
    pairs = [(lat_hbm, lat), (wv_hbm, wv), (emb_hbm, emb)]
    for first in range(0, hidden, wide):
        pairs.append((wh_hbm.at[:, first : first + wide], wh.at[:, first : first + wide]))
    pairs += [(ow_hbm, ow), (nb_hbm, nb_ref), (cf_hbm, cf_ref), (gain_hbm, gain_ref)]
    small = len(pairs) - 4
    copies = [pltpu.make_async_copy(source, target, sems.at[k]) for k, (source, target) in enumerate(pairs)]
    for k in (*range(small + 1, small + 4), *range(small + 1)):
        copies[k].start()
    for copy in copies[small + 1 :]:
        copy.wait()
    rows_of = lax.broadcasted_iota(jnp.int32, (nodes, 256), 0)
    for r in range(points // 256):
        rows = slice(256 * r, 256 * r + 256)
        st = jnp.zeros((nodes, 256), F32)
        for k in range(3):
            st = st + jnp.where(nb_ref[k : k + 1, rows] == rows_of, cf_ref[k : k + 1, rows], 0.0)
        st_ref[:, rows] = st.astype(BF)
    total[...] = jnp.zeros_like(total)
    copies[0].wait()
    copies[1].wait()
    values = dot(lat[...], wv[...]).astype(BF)
    for x in range(4):
        columns = pl.ds(pl.multiple_of(x * 256 + (1 - own["c"]) * 128, 128), 128)
        lat_send[:, 128 * x : 128 * x + 128] = lat[:, columns]
    copies[2].wait()
    for r in range(points // 256):
        rows = slice(256 * r, 256 * r + 256)
        summed = emb[rows, :].astype(F32) + dot(st_ref[:, rows], values, ((0,), (0,)))
        inv = lax.rsqrt(jnp.mean(summed * summed, axis=-1, keepdims=True) + norm_eps)
        inv_ref[rows, :] = inv
        nrm[rows, :] = (summed * inv * gain_ref[...]).astype(BF)
    copies[small].wait()
    for tile in range(hidden // wide):
        copies[3 + tile].wait()
        for r in range(points // 256):
            rows = slice(256 * r, 256 * r + 256)
            for first in range(wide * tile, wide * tile + wide, 256):
                here = slice(first, first + 256)
                pre = dot(nrm[rows, :], wh[:, here])
                pre_ref[rows, here] = pre.astype(BF)
                hid_ref[rows, here] = (pre * cdf_of(pre)).astype(BF)
        here = slice(wide * tile, wide * tile + wide)
        total[0:100, :] += dot(ow[:, here], hid_ref[:, here], ((1,), (1,)))
    for f, m in zip((f0, f1, f2, f3), masks(own["c"])):
        f[...] = total[:, pl.ds(pl.multiple_of((own["x"] ^ m) * 256, 256), 256)]


def slopes_kernel(
    vc_ref, f0, f1, f2, f3, c0, c1, c2, c3, tg_ref, vw_ref, area_ref, s0, s1, s2, s3, held
):
    own = own_place()
    first = pl.multiple_of(own["x"] * 256, 256)
    spread = (1.0 - (1.0 - fair_alpha) / members) / (2.0 * members * (members - 1))
    held[:, 96:112, :] = jnp.zeros((4, 16, 256), F32)
    limit = vc_ref[own["z"] * 4 + own["y"]]
    across = lax.broadcasted_iota(jnp.int32, (104, 100), 1)
    down = lax.broadcasted_iota(jnp.int32, (104, 100), 0)
    weights = jnp.sum(jnp.where(across == down, vw_ref[...], 0.0), axis=1, keepdims=True) * 0.01
    for part in range(2):
        mine = pl.ds(pl.multiple_of(first + 128 * part, 128), 128)
        here = slice(128 * part, 128 * part + 128)
        place = first + 128 * part + lax.broadcasted_iota(jnp.int32, (1, 128), 1)
        live = jnp.where(place < limit, area_ref[:, mine], 0.0)
        for top in range(0, 100, 8):
            rows = slice(top, min(top + 8, 100))
            f = [field[rows, here] for field in (f0, f1, f2, f3, c0, c1, c2, c3)]
            sums = [jnp.zeros_like(f[0]) for _ in range(4)]
            for a in range(4):
                for b in range(a + 1, 8):
                    d = f[a] - f[b]
                    s = d * lax.rsqrt(d * d + kernel_width * kernel_width)
                    sums[a] = sums[a] + s
                    if b < 4:
                        sums[b] = sums[b] - s
            target = tg_ref[rows, mine]
            weight = weights[rows, :] * live
            for a in range(4):
                d = f[a] - target
                s = d * lax.rsqrt(d * d + kernel_width * kernel_width)
                held[a, rows, here] = weight * (s * (1.0 / members) - 2.0 * spread * sums[a])
    for a, s in enumerate((s0, s1, s2, s3)):
        s[...] = held[a].astype(BF)


def gather_slopes(parts, slopes):
    own = own_place()
    for s, m in zip(parts, masks(own["c"])):
        at = pl.ds(pl.multiple_of((own["x"] ^ m) * 256, 256), 256)
        slopes[0:112, at] = s[...]
    slopes[112:128, :] = jnp.zeros((16, slopes.shape[1]), BF)


def out_kernel(s0, s1, s2, s3, hid_ref, go_keep, go_send, slopes, go):
    core = lax.axis_index("core")
    gather_slopes((s0, s1, s2, s3), slopes)
    go[...] = dot(slopes[...], hid_ref[...])
    for x in range(4):
        for ref, c in ((go_keep, core), (go_send, 1 - core)):
            columns = pl.ds(pl.multiple_of(x * 512 + c * 256, 256), 256)
            ref[:, 256 * x : 256 * x + 256] = go[:, columns].astype(BF)


def upper_kernel(
    axis, s0, s1, s2, s3, ow_ref, dg_ref, nrm_ref, pg_ref, keep_ref, send_ref, slopes, own_w, result_0, result_1
):
    points = nrm_ref.shape[0]
    offset = 1024 if axis == "z" else 0
    own = own_place()
    gather_slopes((s0, s1, s2, s3), slopes)
    own_w[96:128, :] = jnp.zeros((32, 1024), BF)
    own_w[0:100, :] = ow_ref[:, offset : offset + 1024]
    for r in range(points // 256):
        rows = slice(256 * r, 256 * r + 256)
        grad = dot(slopes[:, rows], own_w[...], ((0,), (0,)))
        pg_ref[rows, :] = (dg_ref[rows, offset : offset + 1024].astype(F32) * grad).astype(BF)
    for tile, result in enumerate((result_0, result_1)):
        result[...] = dot(nrm_ref[...], pg_ref[:, 512 * tile : 512 * tile + 512], ((0,), (0,)))
        columns = pl.ds(pl.multiple_of((tile ^ (own[axis] & 1)) * 512, 512), 512)
        for ref, core in ((keep_ref, own["c"]), (send_ref, 1 - own["c"])):
            for x in range(4):
                rows = pl.ds(pl.multiple_of(x * 256 + core * 128, 128), 128)
                ref[128 * x : 128 * x + 128, columns] = result[rows, :].astype(BF)


def lower_kernel(pga_ref, pgb_ref, wh_ref, nrm_ref, inv_ref, gain_ref, st_ref, vg_ref, summed):
    nodes, points = st_ref.shape
    gain = gain_ref[...]
    over_gain = 1.0 / gain
    gain_sum = jnp.zeros_like(gain)
    for r in range(points // 256):
        rows = slice(256 * r, 256 * r + 256)
        normed_grad = dot(pga_ref[rows, :], wh_ref[:, 0:1024], ((1,), (1,)))
        normed_grad = normed_grad + dot(pgb_ref[rows, :], wh_ref[:, 1024:2048], ((1,), (1,)))
        normed = nrm_ref[rows, :].astype(F32)
        product = normed_grad * normed
        gain_sum = gain_sum + jnp.sum(product, axis=0, keepdims=True)
        mean = jnp.mean(product, axis=-1, keepdims=True)
        summed_grad = inv_ref[rows, :] * (normed_grad * gain - normed * over_gain * mean)
        summed[rows, :] = summed_grad.astype(BF)
    vg_ref[0:nodes, :] = dot(st_ref[...], summed[...]).astype(BF)
    vg_ref[nodes:, :] = jnp.broadcast_to(gain_sum * over_gain, (16, gain.shape[1])).astype(BF)


def latents_kernel(vg_ref, wv_ref, gl_ref):
    gl_ref[...] = dot(vg_ref[0 : gl_ref.shape[0], :], wv_ref[...], ((1,), (1,))).astype(BF)


def prepare_kernel(lat_ref, go_keep, go_recv, own_lat, out_ref):
    core = lax.axis_index("core")
    for x in range(4):
        columns = pl.ds(pl.multiple_of(x * 256 + core * 128, 128), 128)
        own_lat[:, 128 * x : 128 * x + 128] = lat_ref[:, columns]
    out = (go_keep[...].astype(F32) + go_recv[...].astype(F32)).T.reshape(64, 2, 8, 128)
    for k in range(2):
        out_ref[:, 128 * k : 128 * k + 128] = out[:, k].reshape(512, 128).astype(BF)


def value_kernel(
    own_lat, lat_recv, vg_ref, vg_recv, out_ref, first_ref, second_ref,
    out_hbm, gain_turned, block, sems,
):
    nodes, width = own_lat.shape[0], vg_ref.shape[1]
    variables = 100
    core = lax.axis_index("core")
    copies = [
        pltpu.make_async_copy(first_ref, out_hbm.at[:, 0:512], sems.at[0]),
        pltpu.make_async_copy(second_ref, out_hbm.at[:, 512:1024], sems.at[1]),
        pltpu.make_async_copy(block.at[0:256, :], out_hbm.at[0:256, 1024:], sems.at[2]),
        pltpu.make_async_copy(block.at[256:512, :], out_hbm.at[256:512, 1024:], sems.at[3]),
    ]
    copies[0].start()
    copies[1].start()
    gain = vg_ref[nodes:, :].astype(F32)[0:8] + vg_recv[nodes:, :].astype(F32)[0:8]
    gain_turned[...] = jnp.broadcast_to(gain[0:1], (128, width)).T
    lane = lax.broadcasted_iota(jnp.int32, (128, 128), 1)
    for part in range(2):
        here = slice(256 * part, 256 * part + 256)
        value = dot(own_lat[:, here], vg_ref[0:nodes, :], ((0,), (0,)))
        value = value + dot(lat_recv[:, here], vg_recv[0:nodes, :], ((0,), (0,)))
        block[here, 0:width] = value.astype(BF)
        for x in (2 * part, 2 * part + 1):
            rows = slice(128 * x, 128 * x + 128)
            own_gain = gain_turned[pl.ds(pl.multiple_of(x * 256 + core * 128, 128), 128), :]
            first = out_ref[rows, 0:128].astype(F32)
            block[rows, width : width + 128] = jnp.where(lane == variables, own_gain, first).astype(BF)
        block[here, width + 128 :] = out_ref[here, 128:]
        copies[2 + part].start()
    for copy in copies:
        copy.wait()


def final_kernel(met_ref, value_ref, gain_ref, hidden_ref, out_ref):
    width = value_ref.shape[1]
    first, second = [None, None], [None, None]
    rest = None
    for x in range(4):
        for z in range(4):
            for y in range(4):
                block = met_ref[x * 16 + z * 4 + y].astype(F32)
                for sums, k, columns in ((first, x & 1, slice(0, 512)), (second, z & 1, slice(512, 1024))):
                    sums[k] = block[:, columns] if sums[k] is None else sums[k] + block[:, columns]
                rest = block[:, 1024:] if rest is None else rest + block[:, 1024:]
    for k, part in enumerate(first + second):
        hidden_ref[:, 512 * k : 512 * k + 512] = part
    value_ref[...] = rest[:, :width]
    variables = out_ref.shape[1]
    out_ref[0:8, :] = rest[:, width : width + variables]
    out_ref[8:16, :] = rest[:, width + 128 : width + 128 + variables]
    gain_ref[...] = rest[:, width : width + 128].T[variables : variables + 1]


def cost(flops, moved):
    return pl.CostEstimate(flops=flops, bytes_accessed=moved, transcendentals=0)


def like(shape, dtype=BF):
    return jax.ShapeDtypeStruct(shape, dtype)


def held(*arrays):
    return [pltpu.with_memory_space_constraint(array, pltpu.VMEM) for array in arrays]


def forward(lat, wv, nb, cf, emb, gain, wh, ow):
    nodes, width = lat.shape
    points = emb.shape[0]
    hidden = wh.shape[1]
    vm = pl.BlockSpec(memory_space=pltpu.VMEM)
    raw = pl.BlockSpec(memory_space=pl.ANY)
    args = [pltpu.with_memory_space_constraint(array, pltpu.HBM) for array in (lat, wv, nb, cf, emb, gain, wh, ow)]
    return pl.pallas_call(
        forward_kernel,
        in_specs=[raw] * 8,
        out_specs=[vm] * 10,
        out_shape=[like((104, 256), F32)] * 4
        + [
            pltpu.VMEM((points, hidden), BF), pltpu.VMEM((points, hidden), BF), pltpu.VMEM((points, width), BF),
            pltpu.VMEM((points, 1), F32), pltpu.VMEM((nodes, points), BF), like((nodes, width // 2)),
        ],
        scratch_shapes=[
            pltpu.VMEM((104, points), F32), pltpu.VMEM((nodes, width), BF), pltpu.VMEM((width, width), BF),
            pltpu.VMEM((points, width), BF), pltpu.VMEM((width, hidden), BF), pltpu.VMEM(ow.shape, BF),
            pltpu.VMEM(nb.shape, jnp.int32), pltpu.VMEM(cf.shape, F32), pltpu.VMEM(gain.shape, F32),
            pltpu.SemaphoreType.DMA((7 + hidden // 512,)),
        ],
        compiler_params=pltpu.CompilerParams(vmem_limit_bytes=24 * MIB),
        cost_estimate=cost(6_400_000_000, 12_000_000),
        name="forward",
    )(*args)


def in_vmem(kernel, name, out_shape, scratch, estimate, limit, *args, scalars=0, in_hbm=False):
    vm = pl.BlockSpec(memory_space=pltpu.VMEM)
    many = isinstance(out_shape, list)
    return pl.pallas_call(
        kernel,
        in_specs=[pl.BlockSpec(memory_space=pltpu.SMEM)] * scalars + [vm] * (len(args) - scalars),
        out_specs=[vm] * len(out_shape) if many else pl.BlockSpec(memory_space=pl.ANY) if in_hbm else vm,
        out_shape=out_shape,
        scratch_shapes=scratch,
        compiler_params=pltpu.CompilerParams(vmem_limit_bytes=limit * MIB),
        cost_estimate=estimate,
        name=name,
    )(*args)


def upper(axis, parts, ow, dg, nrm):
    points, width = nrm.shape
    half = like((width // 2, 1024))
    out_shape = [pltpu.VMEM((points, 1024), BF), half, half]
    scratch = [pltpu.VMEM((128, points), BF), pltpu.VMEM((128, 1024), BF)] + [pltpu.VMEM((width, 512), F32)] * 2
    return in_vmem(
        lambda *refs: upper_kernel(axis, *refs), "upper_" + axis, out_shape, scratch, cost(2_700_000_000, 2_000_000), 20,
        *parts, ow, *held(dg, nrm),
    )


def permute(value, pairs):
    return lax.ppermute(value, AXES, pairs)


def total_of(parts, tile):
    return sum(part[:, 512 * tile : 512 * tile + 512].astype(F32) for part in parts)


def per_device(
    latents, grid_embed, neighbours, edge_coef, w_value, gain, w_hidden, output_weight,
    targets, var_weight, area, valid_counts,
):
    lat = latents[0]
    gain_row = gain[None, :]
    f0, f1, f2, f3, hid, pre, nrm, inv, st, lat_send = forward(
        lat, w_value, neighbours, edge_coef, grid_embed, gain_row, w_hidden, output_weight
    )
    core = core_pairs()
    r3 = permute(f3, x_pairs(3))
    r1 = permute(f1, x_pairs(1))
    r2 = permute(f2, x_pairs(2))
    lat_recv = permute(lat_send, core)
    dg = in_vmem(
        gelu_slope_kernel, "gelu_slope", pltpu.VMEM(pre.shape, BF), [], cost(40_000_000, 8_000_000), 16, *held(pre)
    )
    r1, r2, r3, dg = lax.optimization_barrier((r1, r2, r3, dg))
    c0, c1, c2, c3 = (permute(f, core) for f in (f0, r1, r2, r3))
    lat_recv, c0 = lax.optimization_barrier((lat_recv, c0))
    s0, s1, s2, s3 = in_vmem(
        slopes_kernel, "slopes", [like((112, 256))] * 4, [pltpu.VMEM((4, 112, 256), F32)],
        cost(20_000_000, 3_000_000), 16,
        valid_counts, f0, r1, r2, r3, c0, c1, c2, c3, targets, var_weight[None, :], area[None, :], scalars=1,
    )
    q3 = permute(s3, x_pairs(3))
    q1 = permute(s1, x_pairs(1))
    q2 = permute(s2, x_pairs(2))
    parts = [s0, q1, q2, q3]
    pga, *first = upper("x", parts, output_weight, dg, nrm)
    first[1] = permute(first[1], core)
    pga, parts[0] = lax.optimization_barrier((pga, s0))
    pgb, keep, send = upper("z", parts, output_weight, dg, nrm)
    second = [keep, permute(send, core)]
    sent = total_of(first, 1).astype(BF)
    sent_z, s0 = lax.optimization_barrier((total_of(second, 1).astype(BF), s0))
    go_keep, go_send = in_vmem(
        out_kernel, "grad_out", [like((128, 1024)), like((128, 1024))],
        [pltpu.VMEM((128, 1024), BF), pltpu.VMEM((128, 2048), F32)], cost(550_000_000, 1_000_000), 16,
        s0, q1, q2, q3, *held(hid),
    )
    go_send, pgb = lax.optimization_barrier((go_send, pgb))
    go_recv = permute(go_send, core)
    first.append(permute(sent, ring_pairs("x")))
    nodes, width = lat.shape
    vg = in_vmem(
        lower_kernel, "lower", like((nodes + 16, width)), [pltpu.VMEM(nrm.shape, BF)],
        cost(5_100_000_000, 8_000_000), 24,
        *held(pga, pgb), w_hidden, *held(nrm, inv), gain_row, *held(st),
    )
    second.append(permute(sent_z, ring_pairs("z")))
    halves = [total_of(part, 0).astype(BF) for part in (first, second)]
    *halves, vg, go_keep = lax.optimization_barrier((*halves, vg, go_keep))
    own_lat, out = in_vmem(
        prepare_kernel, "prepare", [like((nodes, width // 2)), like((width // 2, 256))], [], cost(1_000_000, 2_000_000), 16,
        lat, go_keep, go_recv,
    )
    vg_recv = permute(vg, core)
    grad_latents = in_vmem(
        latents_kernel, "grad_latents", like(lat.shape), [], cost(800_000_000, 4_000_000), 16, vg, w_value
    )
    mine = in_vmem(
        value_kernel, "grad_value", pltpu.HBM((width // 2, 1024 + width + 256), BF),
        [
            pltpu.VMEM((width, 128), F32), pltpu.VMEM((width // 2, width + 256), BF), pltpu.SemaphoreType.DMA((4,)),
        ],
        cost(800_000_000, 6_000_000), 16,
        own_lat, lat_recv, vg, vg_recv, out, *halves, in_hbm=True,
    )
    sent = mine.reshape(64, 8, mine.shape[1])
    met = lax.all_to_all(sent, CORE_AXES, 0, 0, tiled=True)
    grad_value, grad_gain, grad_hidden, grad_out = in_vmem(
        final_kernel, "final", [like((8, width), F32), like((1, 8), F32), like((8, 2048), F32), like((16, 100), F32)],
        [], cost(2_000_000, 2_600_000), 16, met,
    )
    return (grad_value, grad_gain.reshape(8), grad_hidden, grad_out.T, grad_latents[None])


def solution(mesh):
    mesh = jax.sharding.Mesh(mesh.devices.reshape(4, 2, 4, 4), AXES)
    member, node = ("x", "core"), ("z", "y")
    in_specs = (
        P(member, node, None),
        P(node, None),
        P(None, node),
        P(None, node),
        P(),
        P(),
        P(),
        P(),
        P(None, node),
        P(),
        P(node),
        P(),
    )
    out_specs = (
        P(AXES, None),
        P(AXES),
        P(AXES, None),
        P(None, AXES),
        P(member, node, None),
    )
    return jax.shard_map(
        per_device, mesh=mesh, in_specs=in_specs, out_specs=out_specs, check_vma=False
    )
```

```python
import itertools

import jax
import jax.numpy as jnp
from jax import lax
from jax.experimental import pallas as pl
from jax.experimental.pallas import tpu as pltpu
from jax.sharding import PartitionSpec as P

BF = jnp.bfloat16
F32 = jnp.float32
kernel_width = 0.25
fair_alpha = 0.95
norm_eps = 1e-05
members = 8
GELU_C = 0.7978845608028654
MIB = 1024 * 1024
CORE_AXES = ("x", "z", "y")
AXES = ("x", "core", "z", "y")


def flat(x, c, z, y):
    return ((x * 2 + c) * 4 + z) * 4 + y


def core_pairs():
    return [
        (flat(x, c, z, y), flat(x, 1 - c, z, y))
        for x, c, z, y in itertools.product(range(4), range(2), range(4), range(4))
    ]


def ring_pairs(axis):
    pairs = []
    for x, c, z, y in itertools.product(range(4), range(2), range(4), range(4)):
        to = {"x": x, "z": z, "y": y}
        to[axis] ^= (1, 3)[c]
        pairs.append((flat(x, c, z, y), flat(to["x"], c, to["z"], to["y"])))
    return pairs


def own_place():
    return {"x": lax.axis_index("x"), "c": lax.axis_index("core"), "z": lax.axis_index("z"), "y": lax.axis_index("y")}


def masks(core):
    first, second = 1 + 2 * core, 3 - 2 * core
    return (0, second, first, 2)


def x_pairs(position):
    pairs = []
    for x, c, z, y in itertools.product(range(4), range(2), range(4), range(4)):
        pairs.append((flat(x, c, z, y), flat(x ^ masks(c)[position], c, z, y)))
    return pairs


def dot(a, b, dims=((1,), (0,))):
    return lax.dot_general(a, b, (dims, ((), ())), preferred_element_type=F32)


def cdf_of(pre):
    return 0.5 + 0.5 * jnp.tanh(pre * (GELU_C + (GELU_C * 0.044715) * (pre * pre)))


def gelu_slope_kernel(half, pre_ref, dg_ref):
    columns = slice(1024 * half, 1024 * half + 1024)

    def body(q, carry):
        for part in range(4):
            rows = pl.ds(pl.multiple_of(q * 64 + 16 * part, 16), 16)
            pre = pre_ref[rows, columns].astype(F32)
            square = pre * pre
            t = jnp.tanh(pre * (GELU_C + (GELU_C * 0.044715) * square))
            inner = pre * (GELU_C + (3 * GELU_C * 0.044715) * square)
            dg_ref[rows, :] = ((0.5 + 0.5 * t) * (1.0 + (1.0 - t) * inner)).astype(BF)
        return carry

    lax.fori_loop(0, pre_ref.shape[0] // 64, body, 0)


def forward_kernel(
    lat_hbm, wv_hbm, nb_hbm, cf_hbm, emb_hbm, gain_hbm, wh_hbm, ow_hbm,
    f0, f1, f2, f3, hid_ref, pre_ref, nrm, inv_ref, st_ref, lat_send,
    total, lat, wv, emb, wh, ow, nb_ref, cf_ref, gain_ref, sems,
):
    nodes, points = st_ref.shape
    hidden = wh.shape[1]
    wide = 512
    own = own_place()
    pairs = [(lat_hbm, lat), (wv_hbm, wv), (emb_hbm, emb)]
    for first in range(0, hidden, wide):
        pairs.append((wh_hbm.at[:, first : first + wide], wh.at[:, first : first + wide]))
    pairs += [(ow_hbm, ow), (nb_hbm, nb_ref), (cf_hbm, cf_ref), (gain_hbm, gain_ref)]
    small = len(pairs) - 4
    copies = [pltpu.make_async_copy(source, target, sems.at[k]) for k, (source, target) in enumerate(pairs)]
    for k in (*range(small + 1, small + 4), *range(small + 1)):
        copies[k].start()
    for copy in copies[small + 1 :]:
        copy.wait()
    rows_of = lax.broadcasted_iota(jnp.int32, (nodes, 256), 0)
    for r in range(points // 256):
        rows = slice(256 * r, 256 * r + 256)
        st = jnp.zeros((nodes, 256), F32)
        for k in range(3):
            st = st + jnp.where(nb_ref[k : k + 1, rows] == rows_of, cf_ref[k : k + 1, rows], 0.0)
        st_ref[:, rows] = st.astype(BF)
    total[...] = jnp.zeros_like(total)
    copies[0].wait()
    copies[1].wait()
    values = dot(lat[...], wv[...]).astype(BF)
    for x in range(4):
        columns = pl.ds(pl.multiple_of(x * 256 + (1 - own["c"]) * 128, 128), 128)
        lat_send[:, 128 * x : 128 * x + 128] = lat[:, columns]
    copies[2].wait()
    for r in range(points // 256):
        rows = slice(256 * r, 256 * r + 256)
        summed = emb[rows, :].astype(F32) + dot(st_ref[:, rows], values, ((0,), (0,)))
        inv = lax.rsqrt(jnp.mean(summed * summed, axis=-1, keepdims=True) + norm_eps)
        inv_ref[rows, :] = inv
        nrm[rows, :] = (summed * inv * gain_ref[...]).astype(BF)
    copies[small].wait()
    for tile in range(hidden // wide):
        copies[3 + tile].wait()
        for r in range(points // 256):
            rows = slice(256 * r, 256 * r + 256)
            for first in range(wide * tile, wide * tile + wide, 256):
                here = slice(first, first + 256)
                pre = dot(nrm[rows, :], wh[:, here])
                pre_ref[rows, here] = pre.astype(BF)
                hid_ref[rows, here] = (pre * cdf_of(pre)).astype(BF)
        here = slice(wide * tile, wide * tile + wide)
        total[0:100, :] += dot(ow[:, here], hid_ref[:, here], ((1,), (1,)))
    for f, m in zip((f0, f1, f2, f3), masks(own["c"])):
        f[...] = total[:, pl.ds(pl.multiple_of((own["x"] ^ m) * 256, 256), 256)]


def slopes_kernel(
    vc_ref, f0, f1, f2, f3, c0, c1, c2, c3, tg_ref, vw_ref, area_ref, s0, s1, s2, s3, held
):
    own = own_place()
    first = pl.multiple_of(own["x"] * 256, 256)
    spread = (1.0 - (1.0 - fair_alpha) / members) / (2.0 * members * (members - 1))
    held[:, 96:112, :] = jnp.zeros((4, 16, 256), F32)
    limit = vc_ref[own["z"] * 4 + own["y"]]
    across = lax.broadcasted_iota(jnp.int32, (104, 100), 1)
    down = lax.broadcasted_iota(jnp.int32, (104, 100), 0)
    weights = jnp.sum(jnp.where(across == down, vw_ref[...], 0.0), axis=1, keepdims=True) * 0.01
    for part in range(2):
        mine = pl.ds(pl.multiple_of(first + 128 * part, 128), 128)
        here = slice(128 * part, 128 * part + 128)
        place = first + 128 * part + lax.broadcasted_iota(jnp.int32, (1, 128), 1)
        live = jnp.where(place < limit, area_ref[:, mine], 0.0)
        for top in range(0, 100, 8):
            rows = slice(top, min(top + 8, 100))
            f = [field[rows, here] for field in (f0, f1, f2, f3, c0, c1, c2, c3)]
            sums = [jnp.zeros_like(f[0]) for _ in range(4)]
            for a in range(4):
                for b in range(a + 1, 8):
                    d = f[a] - f[b]
                    s = d * lax.rsqrt(d * d + kernel_width * kernel_width)
                    sums[a] = sums[a] + s
                    if b < 4:
                        sums[b] = sums[b] - s
            target = tg_ref[rows, mine]
            weight = weights[rows, :] * live
            for a in range(4):
                d = f[a] - target
                s = d * lax.rsqrt(d * d + kernel_width * kernel_width)
                held[a, rows, here] = weight * (s * (1.0 / members) - 2.0 * spread * sums[a])
    for a, s in enumerate((s0, s1, s2, s3)):
        s[...] = held[a].astype(BF)


def gather_slopes(parts, slopes):
    own = own_place()
    for s, m in zip(parts, masks(own["c"])):
        at = pl.ds(pl.multiple_of((own["x"] ^ m) * 256, 256), 256)
        slopes[0:112, at] = s[...]
    slopes[112:128, :] = jnp.zeros((16, slopes.shape[1]), BF)


def out_kernel(s0, s1, s2, s3, hid_ref, go_keep, go_send, slopes, go):
    core = lax.axis_index("core")
    gather_slopes((s0, s1, s2, s3), slopes)
    go[...] = dot(slopes[...], hid_ref[...])
    for x in range(4):
        for ref, c in ((go_keep, core), (go_send, 1 - core)):
            columns = pl.ds(pl.multiple_of(x * 512 + c * 256, 256), 256)
            ref[:, 256 * x : 256 * x + 256] = go[:, columns].astype(BF)


def upper_kernel(
    axis, s0, s1, s2, s3, ow_ref, dg_ref, nrm_ref, pg_ref, keep_ref, send_ref, slopes, own_w, result_0, result_1
):
    points = nrm_ref.shape[0]
    offset = 1024 if axis == "z" else 0
    own = own_place()
    gather_slopes((s0, s1, s2, s3), slopes)
    own_w[96:128, :] = jnp.zeros((32, 1024), BF)
    own_w[0:100, :] = ow_ref[:, offset : offset + 1024]
    for r in range(points // 256):
        rows = slice(256 * r, 256 * r + 256)
        grad = dot(slopes[:, rows], own_w[...], ((0,), (0,)))
        pg_ref[rows, :] = (dg_ref[rows, :].astype(F32) * grad).astype(BF)
    for tile, result in enumerate((result_0, result_1)):
        result[...] = dot(nrm_ref[...], pg_ref[:, 512 * tile : 512 * tile + 512], ((0,), (0,)))
        columns = pl.ds(pl.multiple_of((tile ^ (own[axis] & 1)) * 512, 512), 512)
        for ref, core in ((keep_ref, own["c"]), (send_ref, 1 - own["c"])):
            for x in range(4):
                rows = pl.ds(pl.multiple_of(x * 256 + core * 128, 128), 128)
                ref[128 * x : 128 * x + 128, columns] = result[rows, :].astype(BF)


def lower_kernel(pga_ref, pgb_ref, wh_ref, nrm_ref, inv_ref, gain_ref, st_ref, vg_ref, summed):
    nodes, points = st_ref.shape
    gain = gain_ref[...]
    over_gain = 1.0 / gain
    gain_sum = jnp.zeros_like(gain)
    for r in range(points // 256):
        rows = slice(256 * r, 256 * r + 256)
        normed_grad = dot(pga_ref[rows, :], wh_ref[:, 0:1024], ((1,), (1,)))
        normed_grad = normed_grad + dot(pgb_ref[rows, :], wh_ref[:, 1024:2048], ((1,), (1,)))
        normed = nrm_ref[rows, :].astype(F32)
        product = normed_grad * normed
        gain_sum = gain_sum + jnp.sum(product, axis=0, keepdims=True)
        mean = jnp.mean(product, axis=-1, keepdims=True)
        summed_grad = inv_ref[rows, :] * (normed_grad * gain - normed * over_gain * mean)
        summed[rows, :] = summed_grad.astype(BF)
    vg_ref[0:nodes, :] = dot(st_ref[...], summed[...]).astype(BF)
    vg_ref[nodes:, :] = jnp.broadcast_to(gain_sum * over_gain, (16, gain.shape[1])).astype(BF)


def latents_kernel(vg_ref, wv_ref, gl_ref):
    gl_ref[...] = dot(vg_ref[0 : gl_ref.shape[0], :], wv_ref[...], ((1,), (1,))).astype(BF)


def prepare_kernel(lat_ref, go_keep, go_recv, own_lat, out_ref):
    core = lax.axis_index("core")
    for x in range(4):
        columns = pl.ds(pl.multiple_of(x * 256 + core * 128, 128), 128)
        own_lat[:, 128 * x : 128 * x + 128] = lat_ref[:, columns]
    out = (go_keep[...].astype(F32) + go_recv[...].astype(F32)).T.reshape(64, 2, 8, 128)
    for k in range(2):
        out_ref[:, 128 * k : 128 * k + 128] = out[:, k].reshape(512, 128).astype(BF)


def value_kernel(
    own_lat, lat_recv, vg_ref, vg_recv, out_ref, first_ref, second_ref,
    out_hbm, gain_turned, block, sems,
):
    nodes, width = own_lat.shape[0], vg_ref.shape[1]
    variables = 100
    core = lax.axis_index("core")
    copies = [
        pltpu.make_async_copy(first_ref, out_hbm.at[:, 0:512], sems.at[0]),
        pltpu.make_async_copy(second_ref, out_hbm.at[:, 512:1024], sems.at[1]),
        pltpu.make_async_copy(block.at[0:256, :], out_hbm.at[0:256, 1024:], sems.at[2]),
        pltpu.make_async_copy(block.at[256:512, :], out_hbm.at[256:512, 1024:], sems.at[3]),
    ]
    copies[0].start()
    copies[1].start()
    gain = vg_ref[nodes:, :].astype(F32)[0:8] + vg_recv[nodes:, :].astype(F32)[0:8]
    gain_turned[...] = jnp.broadcast_to(gain[0:1], (128, width)).T
    lane = lax.broadcasted_iota(jnp.int32, (128, 128), 1)
    for part in range(2):
        here = slice(256 * part, 256 * part + 256)
        value = dot(own_lat[:, here], vg_ref[0:nodes, :], ((0,), (0,)))
        value = value + dot(lat_recv[:, here], vg_recv[0:nodes, :], ((0,), (0,)))
        block[here, 0:width] = value.astype(BF)
        for x in (2 * part, 2 * part + 1):
            rows = slice(128 * x, 128 * x + 128)
            own_gain = gain_turned[pl.ds(pl.multiple_of(x * 256 + core * 128, 128), 128), :]
            first = out_ref[rows, 0:128].astype(F32)
            block[rows, width : width + 128] = jnp.where(lane == variables, own_gain, first).astype(BF)
        block[here, width + 128 :] = out_ref[here, 128:]
        copies[2 + part].start()
    for copy in copies:
        copy.wait()


def final_kernel(met_ref, value_ref, gain_ref, hidden_ref, out_ref):
    width = value_ref.shape[1]
    first, second = [None, None], [None, None]
    rest = None
    for x in range(4):
        for z in range(4):
            for y in range(4):
                block = met_ref[x * 16 + z * 4 + y].astype(F32)
                for sums, k, columns in ((first, x & 1, slice(0, 512)), (second, z & 1, slice(512, 1024))):
                    sums[k] = block[:, columns] if sums[k] is None else sums[k] + block[:, columns]
                rest = block[:, 1024:] if rest is None else rest + block[:, 1024:]
    for k, part in enumerate(first + second):
        hidden_ref[:, 512 * k : 512 * k + 512] = part
    value_ref[...] = rest[:, :width]
    variables = out_ref.shape[1]
    out_ref[0:8, :] = rest[:, width : width + variables]
    out_ref[8:16, :] = rest[:, width + 128 : width + 128 + variables]
    gain_ref[...] = rest[:, width : width + 128].T[variables : variables + 1]


def cost(flops, moved):
    return pl.CostEstimate(flops=flops, bytes_accessed=moved, transcendentals=0)


def like(shape, dtype=BF):
    return jax.ShapeDtypeStruct(shape, dtype)


def held(*arrays):
    return [pltpu.with_memory_space_constraint(array, pltpu.VMEM) for array in arrays]


def forward(lat, wv, nb, cf, emb, gain, wh, ow):
    nodes, width = lat.shape
    points = emb.shape[0]
    hidden = wh.shape[1]
    vm = pl.BlockSpec(memory_space=pltpu.VMEM)
    raw = pl.BlockSpec(memory_space=pl.ANY)
    args = [pltpu.with_memory_space_constraint(array, pltpu.HBM) for array in (lat, wv, nb, cf, emb, gain, wh, ow)]
    return pl.pallas_call(
        forward_kernel,
        in_specs=[raw] * 8,
        out_specs=[vm] * 10,
        out_shape=[like((104, 256), F32)] * 4
        + [
            pltpu.VMEM((points, hidden), BF), pltpu.VMEM((points, hidden), BF), pltpu.VMEM((points, width), BF),
            pltpu.VMEM((points, 1), F32), pltpu.VMEM((nodes, points), BF), like((nodes, width // 2)),
        ],
        scratch_shapes=[
            pltpu.VMEM((104, points), F32), pltpu.VMEM((nodes, width), BF), pltpu.VMEM((width, width), BF),
            pltpu.VMEM((points, width), BF), pltpu.VMEM((width, hidden), BF), pltpu.VMEM(ow.shape, BF),
            pltpu.VMEM(nb.shape, jnp.int32), pltpu.VMEM(cf.shape, F32), pltpu.VMEM(gain.shape, F32),
            pltpu.SemaphoreType.DMA((7 + hidden // 512,)),
        ],
        compiler_params=pltpu.CompilerParams(vmem_limit_bytes=24 * MIB),
        cost_estimate=cost(6_400_000_000, 12_000_000),
        name="forward",
    )(*args)


def in_vmem(kernel, name, out_shape, scratch, estimate, limit, *args, scalars=0, in_hbm=False):
    vm = pl.BlockSpec(memory_space=pltpu.VMEM)
    many = isinstance(out_shape, list)
    return pl.pallas_call(
        kernel,
        in_specs=[pl.BlockSpec(memory_space=pltpu.SMEM)] * scalars + [vm] * (len(args) - scalars),
        out_specs=[vm] * len(out_shape) if many else pl.BlockSpec(memory_space=pl.ANY) if in_hbm else vm,
        out_shape=out_shape,
        scratch_shapes=scratch,
        compiler_params=pltpu.CompilerParams(vmem_limit_bytes=limit * MIB),
        cost_estimate=estimate,
        name=name,
    )(*args)


def gelu_slope(half, pre):
    return in_vmem(
        lambda *refs: gelu_slope_kernel(half, *refs), f"gelu_slope_{half}", pltpu.VMEM((pre.shape[0], 1024), BF), [],
        cost(20_000_000, 4_000_000), 16, *held(pre),
    )


def upper(axis, parts, ow, dg, nrm):
    points, width = nrm.shape
    half = like((width // 2, 1024))
    out_shape = [pltpu.VMEM((points, 1024), BF), half, half]
    scratch = [pltpu.VMEM((128, points), BF), pltpu.VMEM((128, 1024), BF)] + [pltpu.VMEM((width, 512), F32)] * 2
    return in_vmem(
        lambda *refs: upper_kernel(axis, *refs), "upper_" + axis, out_shape, scratch, cost(2_700_000_000, 2_000_000), 20,
        *parts, ow, *held(dg, nrm),
    )


def permute(value, pairs):
    return lax.ppermute(value, AXES, pairs)


def total_of(parts, tile):
    return sum(part[:, 512 * tile : 512 * tile + 512].astype(F32) for part in parts)


def per_device(
    latents, grid_embed, neighbours, edge_coef, w_value, gain, w_hidden, output_weight,
    targets, var_weight, area, valid_counts,
):
    lat = latents[0]
    gain_row = gain[None, :]
    f0, f1, f2, f3, hid, pre, nrm, inv, st, lat_send = forward(
        lat, w_value, neighbours, edge_coef, grid_embed, gain_row, w_hidden, output_weight
    )
    core = core_pairs()
    r3 = permute(f3, x_pairs(3))
    r1 = permute(f1, x_pairs(1))
    r2 = permute(f2, x_pairs(2))
    lat_recv = permute(lat_send, core)
    dg_x = gelu_slope(0, pre)
    r1, dg_x = lax.optimization_barrier((r1, dg_x))
    c0, c1, c2, c3 = (permute(f, core) for f in (f0, r1, r2, r3))
    lat_recv, c0 = lax.optimization_barrier((lat_recv, c0))
    s0, s1, s2, s3 = in_vmem(
        slopes_kernel, "slopes", [like((112, 256))] * 4, [pltpu.VMEM((4, 112, 256), F32)],
        cost(20_000_000, 3_000_000), 16,
        valid_counts, f0, r1, r2, r3, c0, c1, c2, c3, targets, var_weight[None, :], area[None, :], scalars=1,
    )
    q3 = permute(s3, x_pairs(3))
    q1 = permute(s1, x_pairs(1))
    q2 = permute(s2, x_pairs(2))
    pre, s0 = lax.optimization_barrier((pre, s0))
    dg_z = gelu_slope(1, pre)
    q1, q2, q3, dg_z = lax.optimization_barrier((q1, q2, q3, dg_z))
    parts = [s0, q1, q2, q3]
    pga, *first = upper("x", parts, output_weight, dg_x, nrm)
    first[1] = permute(first[1], core)
    pga, parts[0] = lax.optimization_barrier((pga, s0))
    pgb, keep, send = upper("z", parts, output_weight, dg_z, nrm)
    second = [keep, permute(send, core)]
    sent = total_of(first, 1).astype(BF)
    sent_z, pgb = lax.optimization_barrier((total_of(second, 1).astype(BF), pgb))
    first.append(permute(sent, ring_pairs("x")))
    nodes, width = lat.shape
    vg = in_vmem(
        lower_kernel, "lower", like((nodes + 16, width)), [pltpu.VMEM(nrm.shape, BF)],
        cost(5_100_000_000, 8_000_000), 24,
        *held(pga, pgb), w_hidden, *held(nrm, inv), gain_row, *held(st),
    )
    second.append(permute(sent_z, ring_pairs("z")))
    halves = [total_of(part, 0).astype(BF) for part in (first, second)]
    *halves, vg, s0 = lax.optimization_barrier((*halves, vg, s0))
    vg_recv = permute(vg, core)
    go_keep, go_send = in_vmem(
        out_kernel, "grad_out", [like((128, 1024)), like((128, 1024))],
        [pltpu.VMEM((128, 1024), BF), pltpu.VMEM((128, 2048), F32)], cost(550_000_000, 1_000_000), 16,
        s0, q1, q2, q3, *held(hid),
    )
    go_recv = permute(go_send, core)
    own_lat, out = in_vmem(
        prepare_kernel, "prepare", [like((nodes, width // 2)), like((width // 2, 256))], [], cost(1_000_000, 2_000_000), 16,
        lat, go_keep, go_recv,
    )
    grad_latents = in_vmem(
        latents_kernel, "grad_latents", like(lat.shape), [], cost(800_000_000, 4_000_000), 16, vg, w_value
    )
    mine = in_vmem(
        value_kernel, "grad_value", pltpu.HBM((width // 2, 1024 + width + 256), BF),
        [
            pltpu.VMEM((width, 128), F32), pltpu.VMEM((width // 2, width + 256), BF), pltpu.SemaphoreType.DMA((4,)),
        ],
        cost(800_000_000, 6_000_000), 16,
        own_lat, lat_recv, vg, vg_recv, out, *halves, in_hbm=True,
    )
    sent = mine.reshape(64, 8, mine.shape[1])
    met = lax.all_to_all(sent, CORE_AXES, 0, 0, tiled=True)
    grad_value, grad_gain, grad_hidden, grad_out = in_vmem(
        final_kernel, "final", [like((8, width), F32), like((1, 8), F32), like((8, 2048), F32), like((16, 100), F32)],
        [], cost(2_000_000, 2_600_000), 16, met,
    )
    return (grad_value, grad_gain.reshape(8), grad_hidden, grad_out.T, grad_latents[None])


def solution(mesh):
    mesh = jax.sharding.Mesh(mesh.devices.reshape(4, 2, 4, 4), AXES)
    member, node = ("x", "core"), ("z", "y")
    in_specs = (
        P(member, node, None),
        P(node, None),
        P(None, node),
        P(None, node),
        P(),
        P(),
        P(),
        P(),
        P(None, node),
        P(),
        P(node),
        P(),
    )
    out_specs = (
        P(AXES, None),
        P(AXES),
        P(AXES, None),
        P(None, AXES),
        P(member, node, None),
    )
    return jax.shard_map(
        per_device, mesh=mesh, in_specs=in_specs, out_specs=out_specs, check_vma=False
    )
```

```python
import itertools

import jax
import jax.numpy as jnp
from jax import lax
from jax.experimental import pallas as pl
from jax.experimental.pallas import tpu as pltpu
from jax.sharding import PartitionSpec as P

BF = jnp.bfloat16
F32 = jnp.float32
kernel_width = 0.25
fair_alpha = 0.95
norm_eps = 1e-05
members = 8
GELU_C = 0.7978845608028654
MIB = 1024 * 1024
CORE_AXES = ("x", "z", "y")
AXES = ("x", "core", "z", "y")


def flat(x, c, z, y):
    return ((x * 2 + c) * 4 + z) * 4 + y


def core_pairs():
    return [
        (flat(x, c, z, y), flat(x, 1 - c, z, y))
        for x, c, z, y in itertools.product(range(4), range(2), range(4), range(4))
    ]


def ring_pairs(axis):
    pairs = []
    for x, c, z, y in itertools.product(range(4), range(2), range(4), range(4)):
        to = {"x": x, "z": z, "y": y}
        to[axis] ^= (1, 3)[c]
        pairs.append((flat(x, c, z, y), flat(to["x"], c, to["z"], to["y"])))
    return pairs


def own_place():
    return {"x": lax.axis_index("x"), "c": lax.axis_index("core"), "z": lax.axis_index("z"), "y": lax.axis_index("y")}


def masks(core):
    first, second = 1 + 2 * core, 3 - 2 * core
    return (0, second, first, 2)


def x_pairs(position):
    pairs = []
    for x, c, z, y in itertools.product(range(4), range(2), range(4), range(4)):
        pairs.append((flat(x, c, z, y), flat(x ^ masks(c)[position], c, z, y)))
    return pairs


def dot(a, b, dims=((1,), (0,))):
    return lax.dot_general(a, b, (dims, ((), ())), preferred_element_type=F32)


def cdf_of(pre):
    return 0.5 + 0.5 * jnp.tanh(pre * (GELU_C + (GELU_C * 0.044715) * (pre * pre)))


def gelu_slope_kernel(half, pre_ref, dg_ref):
    columns = slice(1024 * half, 1024 * half + 1024)

    def body(q, carry):
        for part in range(4):
            rows = pl.ds(pl.multiple_of(q * 64 + 16 * part, 16), 16)
            pre = pre_ref[rows, columns].astype(F32)
            square = pre * pre
            t = jnp.tanh(pre * (GELU_C + (GELU_C * 0.044715) * square))
            inner = pre * (GELU_C + (3 * GELU_C * 0.044715) * square)
            dg_ref[rows, :] = ((0.5 + 0.5 * t) * (1.0 + (1.0 - t) * inner)).astype(BF)
        return carry

    lax.fori_loop(0, pre_ref.shape[0] // 64, body, 0)


def forward_kernel(
    lat_hbm, wv_hbm, nb_hbm, cf_hbm, emb_hbm, gain_hbm, wh_hbm, ow,
    f0, f1, f2, f3, hid_ref, pre_ref, nrm, inv_ref, st_ref, lat_send,
    total, lat, wv, emb, wh, nb_ref, cf_ref, gain_ref, sems,
):
    nodes, points = st_ref.shape
    hidden = wh.shape[1]
    wide = 512
    own = own_place()
    pairs = [(lat_hbm, lat), (wv_hbm, wv), (emb_hbm, emb)]
    for first in range(0, hidden, wide):
        pairs.append((wh_hbm.at[:, first : first + wide], wh.at[:, first : first + wide]))
    small = len(pairs)
    pairs += [(nb_hbm, nb_ref), (cf_hbm, cf_ref), (gain_hbm, gain_ref)]
    copies = [pltpu.make_async_copy(source, target, sems.at[k]) for k, (source, target) in enumerate(pairs)]
    for k in (*range(small, small + 3), *range(small)):
        copies[k].start()
    for copy in copies[small:]:
        copy.wait()
    rows_of = lax.broadcasted_iota(jnp.int32, (nodes, 256), 0)
    for r in range(points // 256):
        rows = slice(256 * r, 256 * r + 256)
        st = jnp.zeros((nodes, 256), F32)
        for k in range(3):
            st = st + jnp.where(nb_ref[k : k + 1, rows] == rows_of, cf_ref[k : k + 1, rows], 0.0)
        st_ref[:, rows] = st.astype(BF)
    total[...] = jnp.zeros_like(total)
    copies[0].wait()
    copies[1].wait()
    values = dot(lat[...], wv[...]).astype(BF)
    for x in range(4):
        columns = pl.ds(pl.multiple_of(x * 256 + (1 - own["c"]) * 128, 128), 128)
        lat_send[:, 128 * x : 128 * x + 128] = lat[:, columns]
    copies[2].wait()
    for r in range(points // 256):
        rows = slice(256 * r, 256 * r + 256)
        summed = emb[rows, :].astype(F32) + dot(st_ref[:, rows], values, ((0,), (0,)))
        inv = lax.rsqrt(jnp.mean(summed * summed, axis=-1, keepdims=True) + norm_eps)
        inv_ref[rows, :] = inv
        nrm[rows, :] = (summed * inv * gain_ref[...]).astype(BF)
    for tile in range(hidden // wide):
        copies[3 + tile].wait()
        for r in range(points // 256):
            rows = slice(256 * r, 256 * r + 256)
            for first in range(wide * tile, wide * tile + wide, 256):
                here = slice(first, first + 256)
                pre = dot(nrm[rows, :], wh[:, here])
                pre_ref[rows, here] = pre.astype(BF)
                hid_ref[rows, here] = (pre * cdf_of(pre)).astype(BF)
        here = slice(wide * tile, wide * tile + wide)
        total[0:100, :] += dot(ow[:, here], hid_ref[:, here], ((1,), (1,)))
    for f, m in zip((f0, f1, f2, f3), masks(own["c"])):
        f[...] = total[:, pl.ds(pl.multiple_of((own["x"] ^ m) * 256, 256), 256)]


def slopes_kernel(
    vc_ref, f0, f1, f2, f3, c0, c1, c2, c3, tg_ref, vw_ref, area_ref, s0, s1, s2, s3, held
):
    own = own_place()
    first = pl.multiple_of(own["x"] * 256, 256)
    spread = (1.0 - (1.0 - fair_alpha) / members) / (2.0 * members * (members - 1))
    held[:, 96:112, :] = jnp.zeros((4, 16, 256), F32)
    limit = vc_ref[own["z"] * 4 + own["y"]]
    across = lax.broadcasted_iota(jnp.int32, (104, 100), 1)
    down = lax.broadcasted_iota(jnp.int32, (104, 100), 0)
    weights = jnp.sum(jnp.where(across == down, vw_ref[...], 0.0), axis=1, keepdims=True) * 0.01
    for part in range(2):
        mine = pl.ds(pl.multiple_of(first + 128 * part, 128), 128)
        here = slice(128 * part, 128 * part + 128)
        place = first + 128 * part + lax.broadcasted_iota(jnp.int32, (1, 128), 1)
        live = jnp.where(place < limit, area_ref[:, mine], 0.0)
        for top in range(0, 100, 8):
            rows = slice(top, min(top + 8, 100))
            f = [field[rows, here] for field in (f0, f1, f2, f3, c0, c1, c2, c3)]
            sums = [jnp.zeros_like(f[0]) for _ in range(4)]
            for a in range(4):
                for b in range(a + 1, 8):
                    d = f[a] - f[b]
                    s = d * lax.rsqrt(d * d + kernel_width * kernel_width)
                    sums[a] = sums[a] + s
                    if b < 4:
                        sums[b] = sums[b] - s
            target = tg_ref[rows, mine]
            weight = weights[rows, :] * live
            for a in range(4):
                d = f[a] - target
                s = d * lax.rsqrt(d * d + kernel_width * kernel_width)
                held[a, rows, here] = weight * (s * (1.0 / members) - 2.0 * spread * sums[a])
    for a, s in enumerate((s0, s1, s2, s3)):
        s[...] = held[a].astype(BF)


def gather_slopes(parts, slopes):
    own = own_place()
    for s, m in zip(parts, masks(own["c"])):
        at = pl.ds(pl.multiple_of((own["x"] ^ m) * 256, 256), 256)
        slopes[0:112, at] = s[...]
    slopes[112:128, :] = jnp.zeros((16, slopes.shape[1]), BF)


def out_kernel(s0, s1, s2, s3, hid_ref, go_keep, go_send, slopes, go):
    core = lax.axis_index("core")
    gather_slopes((s0, s1, s2, s3), slopes)
    go[...] = dot(slopes[...], hid_ref[...])
    for x in range(4):
        for ref, c in ((go_keep, core), (go_send, 1 - core)):
            columns = pl.ds(pl.multiple_of(x * 512 + c * 256, 256), 256)
            ref[:, 256 * x : 256 * x + 256] = go[:, columns].astype(BF)


def upper_kernel(
    axis, s0, s1, s2, s3, ow_ref, dg_ref, nrm_ref, pg_ref, keep_ref, send_ref, slopes, own_w, result_0, result_1
):
    points = nrm_ref.shape[0]
    offset = 1024 if axis == "z" else 0
    own = own_place()
    gather_slopes((s0, s1, s2, s3), slopes)
    own_w[96:128, :] = jnp.zeros((32, 1024), BF)
    own_w[0:100, :] = ow_ref[:, offset : offset + 1024]
    for r in range(points // 256):
        rows = slice(256 * r, 256 * r + 256)
        grad = dot(slopes[:, rows], own_w[...], ((0,), (0,)))
        pg_ref[rows, :] = (dg_ref[rows, :].astype(F32) * grad).astype(BF)
    for tile, result in enumerate((result_0, result_1)):
        result[...] = dot(nrm_ref[...], pg_ref[:, 512 * tile : 512 * tile + 512], ((0,), (0,)))
        columns = pl.ds(pl.multiple_of((tile ^ (own[axis] & 1)) * 512, 512), 512)
        for ref, core in ((keep_ref, own["c"]), (send_ref, 1 - own["c"])):
            for x in range(4):
                rows = pl.ds(pl.multiple_of(x * 256 + core * 128, 128), 128)
                ref[128 * x : 128 * x + 128, columns] = result[rows, :].astype(BF)


def lower_kernel(pga_ref, pgb_ref, wh_ref, nrm_ref, inv_ref, gain_ref, st_ref, vg_ref, summed):
    nodes, points = st_ref.shape
    gain = gain_ref[...]
    over_gain = 1.0 / gain
    gain_sum = jnp.zeros_like(gain)
    for r in range(points // 256):
        rows = slice(256 * r, 256 * r + 256)
        normed_grad = dot(pga_ref[rows, :], wh_ref[:, 0:1024], ((1,), (1,)))
        normed_grad = normed_grad + dot(pgb_ref[rows, :], wh_ref[:, 1024:2048], ((1,), (1,)))
        normed = nrm_ref[rows, :].astype(F32)
        product = normed_grad * normed
        gain_sum = gain_sum + jnp.sum(product, axis=0, keepdims=True)
        mean = jnp.mean(product, axis=-1, keepdims=True)
        summed_grad = inv_ref[rows, :] * (normed_grad * gain - normed * over_gain * mean)
        summed[rows, :] = summed_grad.astype(BF)
    vg_ref[0:nodes, :] = dot(st_ref[...], summed[...]).astype(BF)
    vg_ref[nodes:, :] = jnp.broadcast_to(gain_sum * over_gain, (16, gain.shape[1])).astype(BF)


def latents_kernel(vg_ref, wv_ref, gl_ref):
    gl_ref[...] = dot(vg_ref[0 : gl_ref.shape[0], :], wv_ref[...], ((1,), (1,))).astype(BF)


def prepare_kernel(lat_ref, go_keep, go_recv, own_lat, out_ref):
    core = lax.axis_index("core")
    for x in range(4):
        columns = pl.ds(pl.multiple_of(x * 256 + core * 128, 128), 128)
        own_lat[:, 128 * x : 128 * x + 128] = lat_ref[:, columns]
    out = (go_keep[...].astype(F32) + go_recv[...].astype(F32)).T.reshape(64, 2, 8, 128)
    for k in range(2):
        out_ref[:, 128 * k : 128 * k + 128] = out[:, k].reshape(512, 128).astype(BF)


def value_kernel(
    own_lat, lat_recv, vg_ref, vg_recv, out_ref, first_ref, second_ref,
    out_hbm, gain_turned, block, sems,
):
    nodes, width = own_lat.shape[0], vg_ref.shape[1]
    variables = 100
    core = lax.axis_index("core")
    copies = [
        pltpu.make_async_copy(first_ref, out_hbm.at[:, 0:512], sems.at[0]),
        pltpu.make_async_copy(second_ref, out_hbm.at[:, 512:1024], sems.at[1]),
        pltpu.make_async_copy(block.at[0:256, :], out_hbm.at[0:256, 1024:], sems.at[2]),
        pltpu.make_async_copy(block.at[256:512, :], out_hbm.at[256:512, 1024:], sems.at[3]),
    ]
    copies[0].start()
    copies[1].start()
    gain = vg_ref[nodes:, :].astype(F32)[0:8] + vg_recv[nodes:, :].astype(F32)[0:8]
    gain_turned[...] = jnp.broadcast_to(gain[0:1], (128, width)).T
    lane = lax.broadcasted_iota(jnp.int32, (128, 128), 1)
    for part in range(2):
        here = slice(256 * part, 256 * part + 256)
        value = dot(own_lat[:, here], vg_ref[0:nodes, :], ((0,), (0,)))
        value = value + dot(lat_recv[:, here], vg_recv[0:nodes, :], ((0,), (0,)))
        block[here, 0:width] = value.astype(BF)
        for x in (2 * part, 2 * part + 1):
            rows = slice(128 * x, 128 * x + 128)
            own_gain = gain_turned[pl.ds(pl.multiple_of(x * 256 + core * 128, 128), 128), :]
            first = out_ref[rows, 0:128].astype(F32)
            block[rows, width : width + 128] = jnp.where(lane == variables, own_gain, first).astype(BF)
        block[here, width + 128 :] = out_ref[here, 128:]
        copies[2 + part].start()
    for copy in copies:
        copy.wait()


def final_kernel(met_ref, value_ref, gain_ref, hidden_ref, out_ref):
    width = value_ref.shape[1]
    first, second = [None, None], [None, None]
    rest = None
    for x in range(4):
        for z in range(4):
            for y in range(4):
                source = x * 16 + z * 4 + y
                if source % 2 == 0:
                    two = met_ref[8 * source : 8 * source + 16, :].astype(F32)
                block = two[0:8] if source % 2 == 0 else two[8:16]
                for sums, k, columns in ((first, x & 1, slice(0, 512)), (second, z & 1, slice(512, 1024))):
                    sums[k] = block[:, columns] if sums[k] is None else sums[k] + block[:, columns]
                rest = block[:, 1024:] if rest is None else rest + block[:, 1024:]
    for k, part in enumerate(first + second):
        hidden_ref[:, 512 * k : 512 * k + 512] = part
    value_ref[...] = rest[:, :width]
    variables = out_ref.shape[1]
    out_ref[0:8, :] = rest[:, width : width + variables]
    out_ref[8:16, :] = rest[:, width + 128 : width + 128 + variables]
    gain_ref[...] = rest[:, width : width + 128].T[variables : variables + 1]


def cost(flops, moved):
    return pl.CostEstimate(flops=flops, bytes_accessed=moved, transcendentals=0)


def like(shape, dtype=BF):
    return jax.ShapeDtypeStruct(shape, dtype)


def held(*arrays):
    return [pltpu.with_memory_space_constraint(array, pltpu.VMEM) for array in arrays]


def forward(lat, wv, nb, cf, emb, gain, wh, ow):
    nodes, width = lat.shape
    points = emb.shape[0]
    hidden = wh.shape[1]
    vm = pl.BlockSpec(memory_space=pltpu.VMEM)
    raw = pl.BlockSpec(memory_space=pl.ANY)
    args = [pltpu.with_memory_space_constraint(array, pltpu.HBM) for array in (lat, wv, nb, cf, emb, gain, wh)]
    return pl.pallas_call(
        forward_kernel,
        in_specs=[raw] * 7 + [vm],
        out_specs=[vm] * 10,
        out_shape=[like((104, 256), F32)] * 4
        + [
            pltpu.VMEM((points, hidden), BF), pltpu.VMEM((points, hidden), BF), pltpu.VMEM((points, width), BF),
            pltpu.VMEM((points, 1), F32), pltpu.VMEM((nodes, points), BF), like((nodes, width // 2)),
        ],
        scratch_shapes=[
            pltpu.VMEM((104, points), F32), pltpu.VMEM((nodes, width), BF), pltpu.VMEM((width, width), BF),
            pltpu.VMEM((points, width), BF), pltpu.VMEM((width, hidden), BF),
            pltpu.VMEM(nb.shape, jnp.int32), pltpu.VMEM(cf.shape, F32), pltpu.VMEM(gain.shape, F32),
            pltpu.SemaphoreType.DMA((6 + hidden // 512,)),
        ],
        compiler_params=pltpu.CompilerParams(vmem_limit_bytes=24 * MIB),
        cost_estimate=cost(6_400_000_000, 12_000_000),
        name="forward",
    )(*args, ow)


def in_vmem(kernel, name, out_shape, scratch, estimate, limit, *args, scalars=0, in_hbm=False):
    vm = pl.BlockSpec(memory_space=pltpu.VMEM)
    many = isinstance(out_shape, list)
    return pl.pallas_call(
        kernel,
        in_specs=[pl.BlockSpec(memory_space=pltpu.SMEM)] * scalars + [vm] * (len(args) - scalars),
        out_specs=[vm] * len(out_shape) if many else pl.BlockSpec(memory_space=pl.ANY) if in_hbm else vm,
        out_shape=out_shape,
        scratch_shapes=scratch,
        compiler_params=pltpu.CompilerParams(vmem_limit_bytes=limit * MIB),
        cost_estimate=estimate,
        name=name,
    )(*args)


def gelu_slope(half, pre):
    return in_vmem(
        lambda *refs: gelu_slope_kernel(half, *refs), f"gelu_slope_{half}", pltpu.VMEM((pre.shape[0], 1024), BF), [],
        cost(20_000_000, 4_000_000), 16, *held(pre),
    )


def upper(axis, parts, ow, dg, nrm):
    points, width = nrm.shape
    half = like((width // 2, 1024))
    out_shape = [pltpu.VMEM((points, 1024), BF), half, half]
    scratch = [pltpu.VMEM((128, points), BF), pltpu.VMEM((128, 1024), BF)] + [pltpu.VMEM((width, 512), F32)] * 2
    return in_vmem(
        lambda *refs: upper_kernel(axis, *refs), "upper_" + axis, out_shape, scratch, cost(2_700_000_000, 2_000_000), 20,
        *parts, ow, *held(dg, nrm),
    )


def permute(value, pairs):
    return lax.ppermute(value, AXES, pairs)


def total_of(parts, tile):
    return sum(part[:, 512 * tile : 512 * tile + 512].astype(F32) for part in parts)


def per_device(
    latents, grid_embed, neighbours, edge_coef, w_value, gain, w_hidden, output_weight,
    targets, var_weight, area, valid_counts,
):
    lat = latents[0]
    gain_row = gain[None, :]
    f0, f1, f2, f3, hid, pre, nrm, inv, st, lat_send = forward(
        lat, w_value, neighbours, edge_coef, grid_embed, gain_row, w_hidden, output_weight
    )
    core = core_pairs()
    r3 = permute(f3, x_pairs(3))
    r1 = permute(f1, x_pairs(1))
    r2 = permute(f2, x_pairs(2))
    lat_recv = permute(lat_send, core)
    dg_x = gelu_slope(0, pre)
    r1, dg_x = lax.optimization_barrier((r1, dg_x))
    c0, c1, c2, c3 = (permute(f, core) for f in (f0, r1, r2, r3))
    lat_recv, c0 = lax.optimization_barrier((lat_recv, c0))
    s0, s1, s2, s3 = in_vmem(
        slopes_kernel, "slopes", [like((112, 256))] * 4, [pltpu.VMEM((4, 112, 256), F32)],
        cost(20_000_000, 3_000_000), 16,
        valid_counts, f0, r1, r2, r3, c0, c1, c2, c3, targets, var_weight[None, :], area[None, :], scalars=1,
    )
    q3 = permute(s3, x_pairs(3))
    q1 = permute(s1, x_pairs(1))
    q2 = permute(s2, x_pairs(2))
    pre, s0 = lax.optimization_barrier((pre, s0))
    dg_z = gelu_slope(1, pre)
    q1, q2, q3, dg_z = lax.optimization_barrier((q1, q2, q3, dg_z))
    parts = [s0, q1, q2, q3]
    pga, *first = upper("x", parts, output_weight, dg_x, nrm)
    first[1] = permute(first[1], core)
    pga, parts[0] = lax.optimization_barrier((pga, s0))
    pgb, keep, send = upper("z", parts, output_weight, dg_z, nrm)
    second = [keep, permute(send, core)]
    sent = total_of(first, 1).astype(BF)
    sent_z, pgb = lax.optimization_barrier((total_of(second, 1).astype(BF), pgb))
    first.append(permute(sent, ring_pairs("x")))
    nodes, width = lat.shape
    vg = in_vmem(
        lower_kernel, "lower", like((nodes + 16, width)), [pltpu.VMEM(nrm.shape, BF)],
        cost(5_100_000_000, 8_000_000), 24,
        *held(pga, pgb), w_hidden, *held(nrm, inv), gain_row, *held(st),
    )
    second.append(permute(sent_z, ring_pairs("z")))
    halves = [total_of(part, 0).astype(BF) for part in (first, second)]
    *halves, vg, s0 = lax.optimization_barrier((*halves, vg, s0))
    vg_recv = permute(vg, core)
    go_keep, go_send = in_vmem(
        out_kernel, "grad_out", [like((128, 1024)), like((128, 1024))],
        [pltpu.VMEM((128, 1024), BF), pltpu.VMEM((128, 2048), F32)], cost(550_000_000, 1_000_000), 16,
        s0, q1, q2, q3, *held(hid),
    )
    go_recv = permute(go_send, core)
    own_lat, out = in_vmem(
        prepare_kernel, "prepare", [like((nodes, width // 2)), like((width // 2, 256))], [], cost(1_000_000, 2_000_000), 16,
        lat, go_keep, go_recv,
    )
    grad_latents = in_vmem(
        latents_kernel, "grad_latents", like(lat.shape), [], cost(800_000_000, 4_000_000), 16, vg, w_value
    )
    mine = in_vmem(
        value_kernel, "grad_value", pltpu.HBM((width // 2, 1024 + width + 256), BF),
        [
            pltpu.VMEM((width, 128), F32), pltpu.VMEM((width // 2, width + 256), BF), pltpu.SemaphoreType.DMA((4,)),
        ],
        cost(800_000_000, 6_000_000), 16,
        own_lat, lat_recv, vg, vg_recv, out, *halves, in_hbm=True,
    )
    sent = mine.reshape(64, 8, mine.shape[1])
    met = lax.all_to_all(sent, CORE_AXES, 0, 0, tiled=True)
    grad_value, grad_gain, grad_hidden, grad_out = in_vmem(
        final_kernel, "final", [like((8, width), F32), like((1, 8), F32), like((8, 2048), F32), like((16, 100), F32)],
        [], cost(2_000_000, 2_600_000), 16, met.reshape(mine.shape),
    )
    return (grad_value, grad_gain.reshape(8), grad_hidden, grad_out.T, grad_latents[None])


def solution(mesh):
    mesh = jax.sharding.Mesh(mesh.devices.reshape(4, 2, 4, 4), AXES)
    member, node = ("x", "core"), ("z", "y")
    in_specs = (
        P(member, node, None),
        P(node, None),
        P(None, node),
        P(None, node),
        P(),
        P(),
        P(),
        P(),
        P(None, node),
        P(),
        P(node),
        P(),
    )
    out_specs = (
        P(AXES, None),
        P(AXES),
        P(AXES, None),
        P(None, AXES),
        P(member, node, None),
    )
    return jax.shard_map(
        per_device, mesh=mesh, in_specs=in_specs, out_specs=out_specs, check_vma=False
    )
```
